32 devices in a mesh: node: 4 (over x, core), chip: 8 (over z, y).
Axes of the slice: x: 2, y: 2, z: 4, core: 2. Of those that a mesh axis runs over, the one named last changes fastest.
Arguments:
- tokens: bfloat16 [128, 145, 1024], P(('node', 'chip')), may hold values from -6 to 6
- cotangent: bfloat16 [128, 145, 1024], P(('node', 'chip')), may hold values from -6 to 6
- w_attn_in: float32 [2, 1024, 3072], P(None, ('node', 'chip')), may hold values from -0.1875 to 0.1875
- w_attn_out: float32 [2, 1024, 1024], P(None, ('node', 'chip')), may hold values from -0.5 to 0.5
- w_mlp_in: float32 [2, 1024, 4096], P(None, ('node', 'chip')), may hold values from -0.1875 to 0.1875
- w_mlp_out: float32 [2, 4096, 1024], P(None, ('node', 'chip')), may hold values from -0.09375 to 0.09375
- vectors: float32 [2, 14336], P(None, ('node', 'chip')), may hold values from -1.5 to 1.5
- first_attn_in: float32 [2, 1024, 3072], P(None, ('node', 'chip')), may hold values from -28 to 28
- first_attn_out: float32 [2, 1024, 1024], P(None, ('node', 'chip')), may hold values from -28 to 28
- first_mlp_in: float32 [2, 1024, 4096], P(None, ('node', 'chip')), may hold values from -32 to 32
- first_mlp_out: float32 [2, 4096, 1024], P(None, ('node', 'chip')), may hold values from -64 to 64
- first_vectors: float32 [2, 14336], P(None, ('node', 'chip')), may hold values from -96 to 96
- second_attn_in: float32 [2, 1024, 3072], P(None, ('node', 'chip')), may hold values from 0.8352 to 13.3632
- second_attn_out: float32 [2, 1024, 1024], P(None, ('node', 'chip')), may hold values from 0.8352 to 13.3632
- second_mlp_in: float32 [2, 1024, 4096], P(None, ('node', 'chip')), may hold values from 1.1368 to 18.1888
- second_mlp_out: float32 [2, 4096, 1024], P(None, ('node', 'chip')), may hold values from 4.5472 to 72.7552
- second_vectors: float32 [2, 14336], P(None, ('node', 'chip')), may hold values from 9.28 to 148.48
Outputs:
- output: bfloat16 [128, 145, 1024], P(('node', 'chip'))
- d_tokens: float32 [128, 145, 1024], P(('node', 'chip'))
- new_attn_in: float32 [2, 1024, 3072], P(None, ('node', 'chip'))
- new_attn_out: float32 [2, 1024, 1024], P(None, ('node', 'chip'))
- new_mlp_in: float32 [2, 1024, 4096], P(None, ('node', 'chip'))
- new_mlp_out: float32 [2, 4096, 1024], P(None, ('node', 'chip'))
- new_vectors: float32 [2, 14336], P(None, ('node', 'chip'))
- new_first_attn_in: float32 [2, 1024, 3072], P(None, ('node', 'chip'))
- new_first_attn_out: float32 [2, 1024, 1024], P(None, ('node', 'chip'))
- new_first_mlp_in: float32 [2, 1024, 4096], P(None, ('node', 'chip'))
- new_first_mlp_out: float32 [2, 4096, 1024], P(None, ('node', 'chip'))
- new_first_vectors: float32 [2, 14336], P(None, ('node', 'chip'))
- new_second_attn_in: float32 [2, 1024, 3072], P(None, ('node', 'chip'))
- new_second_attn_out: float32 [2, 1024, 1024], P(None, ('node', 'chip'))
- new_second_mlp_in: float32 [2, 1024, 4096], P(None, ('node', 'chip'))
- new_second_mlp_out: float32 [2, 4096, 1024], P(None, ('node', 'chip'))
- new_second_vectors: float32 [2, 14336], P(None, ('node', 'chip'))
The draws below stay inside these ranges and needn't reach their ends.
All inputs are finite; a program needn't handle non-finite values.
Results may differ from the reference program's by a relative error of at most 0.012.
The reference program's roundings to bfloat16 on the way count: a program that leaves them out, or rounds other values in their place, can miss the bound.
Values may be sent and summed in bfloat16 or wider, within the bound.
A program may use at most 320 MiB of HBM per device.

```python
import math
import jax
import jax.numpy as jnp
from jax import lax

D = 1024
HEADS = 16
HEAD_DIM = 64
FF = 4096
LAYERS = 2
STEP = 10
SEQ = 145
IMAGES = 128
VECS = 14336


def draw_vectors(key, part):
    key = jax.random.fold_in(key, 11)
    gain_key, shift_key = jax.random.split(key)
    gains = jax.random.uniform(gain_key, (LAYERS, VECS), jnp.float32, 0.5, 1.5)
    shifts = jnp.clip(0.3 * jax.random.normal(shift_key, (LAYERS, VECS), jnp.float32), -1.5, 1.5)
    row_index = jnp.arange(VECS) // D
    is_gain = (row_index == 0) | (row_index == 5) | (row_index == 6) | (row_index == 9)
    return jnp.where(is_gain[None, :], gains, shifts)


def block_levels(key, shape, cuts, low, top_value):
    def one(axis_at, blocks):
        steps = jax.random.uniform(jax.random.fold_in(jax.random.fold_in(key, 6), axis_at), (blocks,), jnp.float32, low / len(cuts), top_value / len(cuts))
        return jnp.repeat(jnp.exp(steps), shape[axis_at] // blocks).reshape((-1,) + (1,) * (len(shape) - axis_at - 1))

    gain = one(*cuts[0])
    for cut in cuts[1:]:
        gain = gain * one(*cut)
    return gain


def scatter_about(own_key, dims, width, reach, cuts=(), dtype=jnp.bfloat16):
    loudness = block_levels(own_key, dims, cuts, -0.22, 0.18) if cuts else 1.0
    drawn = jax.random.normal(own_key, dims, jnp.float32) * width * loudness
    return jnp.minimum(jnp.maximum(drawn, -reach), reach).astype(dtype)


def setup_inputs(seed: int = 0) -> dict:
    seeds = jax.random.split(jax.random.key(seed), 18)
    tokens = scatter_about(seeds[0], (IMAGES, SEQ, D), 1.0, 6.0, ((0, 32),))
    cotangent = scatter_about(seeds[1], (IMAGES, SEQ, D), 1.0, 6.0, ((0, 32),))
    w_attn_in = scatter_about(seeds[2], (LAYERS, D, 3 * D), D ** -0.5, 0.1875, ((1, 32),), jnp.float32)
    w_attn_out = scatter_about(seeds[3], (LAYERS, D, D), (D // 8) ** -0.5, 0.5, ((1, 32),), jnp.float32)
    w_mlp_in = scatter_about(seeds[4], (LAYERS, D, FF), D ** -0.5, 0.1875, ((1, 32),), jnp.float32)
    w_mlp_out = scatter_about(seeds[5], (LAYERS, FF, D), FF ** -0.5, 0.09375, ((1, 32),), jnp.float32)
    vectors = draw_vectors(jax.random.fold_in(seeds[17], 71), 0)
    first_attn_in = scatter_about(seeds[7], (LAYERS, D, 3 * D), (0.111 * 0.3 * (IMAGES * SEQ) ** 0.5), 28.0, ((1, 32),), jnp.float32)
    first_attn_out = scatter_about(seeds[8], (LAYERS, D, D), (0.111 * 0.3 * (IMAGES * SEQ) ** 0.5), 28.0, ((1, 32),), jnp.float32)
    first_mlp_in = scatter_about(seeds[9], (LAYERS, D, FF), (0.111 * 0.35 * (IMAGES * SEQ) ** 0.5), 32.0, ((1, 32),), jnp.float32)
    first_mlp_out = scatter_about(seeds[10], (LAYERS, FF, D), (0.111 * 0.7 * (IMAGES * SEQ) ** 0.5), 64.0, ((1, 32),), jnp.float32)
    first_vectors = scatter_about(seeds[11], (LAYERS, VECS), (0.111 * (IMAGES * SEQ) ** 0.5), 96.0, ((1, 32),), jnp.float32)
    second_attn_in = jnp.clip(jnp.exp(math.log(13.3632) - 2.7725887 * jax.random.uniform(seeds[12], (LAYERS, D, 3 * D), jnp.float32) ** block_levels(seeds[12], (LAYERS, D, 3 * D), ((1, 32),), -0.2, 0.2)), 0.8352, 13.3632)
    second_attn_out = jnp.clip(jnp.exp(math.log(13.3632) - 2.7725887 * jax.random.uniform(seeds[13], (LAYERS, D, D), jnp.float32) ** block_levels(seeds[13], (LAYERS, D, D), ((1, 32),), -0.2, 0.2)), 0.8352, 13.3632)
    second_mlp_in = jnp.clip(jnp.exp(math.log(18.1888) - 2.7725887 * jax.random.uniform(seeds[14], (LAYERS, D, FF), jnp.float32) ** block_levels(seeds[14], (LAYERS, D, FF), ((1, 32),), -0.2, 0.2)), 1.1368, 18.1888)
    second_mlp_out = jnp.clip(jnp.exp(math.log(72.7552) - 2.7725887 * jax.random.uniform(seeds[15], (LAYERS, FF, D), jnp.float32) ** block_levels(seeds[15], (LAYERS, FF, D), ((1, 32),), -0.2, 0.2)), 4.5472, 72.7552)
    second_vectors = jnp.clip(jnp.exp(math.log(148.48) - 2.7725887 * jax.random.uniform(seeds[16], (LAYERS, VECS), jnp.float32) ** block_levels(seeds[16], (LAYERS, VECS), ((1, 32),), -0.2, 0.2)), 9.28, 148.48)
    return dict(tokens=tokens, cotangent=cotangent, w_attn_in=w_attn_in, w_attn_out=w_attn_out, w_mlp_in=w_mlp_in, w_mlp_out=w_mlp_out, vectors=vectors, first_attn_in=first_attn_in, first_attn_out=first_attn_out, first_mlp_in=first_mlp_in, first_mlp_out=first_mlp_out, first_vectors=first_vectors, second_attn_in=second_attn_in, second_attn_out=second_attn_out, second_mlp_in=second_mlp_in, second_mlp_out=second_mlp_out, second_vectors=second_vectors)


@jax.custom_vjp
def low(v):
    return lax.optimization_barrier(v.astype(jnp.bfloat16)).astype(jnp.float32)

@jax.custom_vjp
def low_back(v):
    return v

def low_keep(v):
    return (low(v), None)

def low_pass(kept, grad):
    return (grad,)

def back_keep(v):
    return (v, None)

def back_low(kept, grad):
    return (low(grad),)
low.defvjp(low_keep, low_pass)
low_back.defvjp(back_keep, back_low)
precise = lax.Precision.HIGHEST
norm_eps = 1e-06
beta_first = 0.9
beta_second = 0.999
adam_eps = 1e-08

def layer_norm(values, gain_row, shift_row):
    centre = lax.optimization_barrier(jnp.mean(values, axis=-1, keepdims=True))
    centred = values - centre
    spread = lax.optimization_barrier(jnp.mean(centred * centred, axis=-1, keepdims=True))
    return centred * lax.rsqrt(spread + norm_eps) * gain_row + shift_row

def one_layer(hidden, w_in, w_out, w_up, w_down, vector_row):
    groups = hidden.shape[0]
    pieces = [vector_row[index * D:(index + 1) * D] for index in range(10)]
    gain_a, shift_a, bias_q, bias_v, bias_o, scale_a, gain_m, shift_m, bias_d, scale_m = pieces
    bias_u = vector_row[10 * D:]
    normed_a = low(layer_norm(hidden, gain_a, shift_a))
    projected = low_back(jnp.einsum('gsd,de->gse', normed_a, w_in, precision=precise))
    projected = projected + jnp.concatenate([bias_q, jnp.zeros((D,), jnp.float32), bias_v])
    heads_shape = (groups, SEQ, HEADS, HEAD_DIM)
    query = low(projected[..., :D]).reshape(heads_shape)
    keys = low(projected[..., D:2 * D]).reshape(heads_shape)
    values = low(projected[..., 2 * D:]).reshape(heads_shape)
    raw = jnp.einsum('gqhc,gkhc->ghqk', query, keys, precision=precise) * HEAD_DIM ** (-0.5)
    scores = low_back(raw)
    top_score = lax.optimization_barrier(jnp.max(scores, axis=-1, keepdims=True))
    expo = jnp.exp(scores - top_score)
    probs = low(expo / lax.optimization_barrier(jnp.sum(expo, axis=-1, keepdims=True)))
    mixed = jnp.einsum('ghqk,gkhc->gqhc', probs, values, precision=precise).reshape(groups, SEQ, D)
    mixed = low(low_back(mixed))
    branch = low_back(jnp.einsum('gsd,de->gse', mixed, w_out, precision=precise)) + bias_o
    middle = hidden + scale_a * branch
    normed_m = low(layer_norm(middle, gain_m, shift_m))
    upper = low_back(jnp.einsum('gsd,df->gsf', normed_m, w_up, precision=precise)) + bias_u
    active = low(jax.nn.gelu(upper, approximate=False))
    down = low_back(jnp.einsum('gsf,fd->gsd', active, w_down, precision=precise)) + bias_d
    return middle + scale_m * down

def network(tokens, w_attn_in, w_attn_out, w_mlp_in, w_mlp_out, vectors):
    rounded = (low(w_attn_in), low(w_attn_out), low(w_mlp_in), low(w_mlp_out), low(vectors))
    group = math.gcd(IMAGES, 16)
    blocks = tokens.reshape(IMAGES // group, group, SEQ, D)

    def run_block(block):
        hidden = block
        for layer_index in range(LAYERS):
            hidden = one_layer(hidden, rounded[0][layer_index], rounded[1][layer_index], rounded[2][layer_index], rounded[3][layer_index], rounded[4][layer_index])
        return hidden
    result = lax.map(jax.checkpoint(run_block), blocks)
    return result.reshape(IMAGES, SEQ, D)

def adamw(weight, gradient, first, second, rate, decay):
    first_new = beta_first * first + (1.0 - beta_first) * gradient
    second_new = beta_second * second + (1.0 - beta_second) * gradient * gradient
    fix_first = 1.0 - beta_first ** STEP
    fix_second = 1.0 - beta_second ** STEP
    stepped = first_new / fix_first / (jnp.sqrt(second_new / fix_second) + adam_eps)
    return (weight - rate * (stepped + decay * weight), first_new, second_new)

def reference(tokens, cotangent, w_attn_in, w_attn_out, w_mlp_in, w_mlp_out, vectors, first_attn_in, first_attn_out, first_mlp_in, first_mlp_out, first_vectors, second_attn_in, second_attn_out, second_mlp_in, second_mlp_out, second_vectors):
    params = (w_attn_in, w_attn_out, w_mlp_in, w_mlp_out, vectors)
    result, pullback = jax.vjp(network, tokens.astype(jnp.float32), *params)
    gradients = pullback(cotangent.astype(jnp.float32))
    firsts = (first_attn_in, first_attn_out, first_mlp_in, first_mlp_out, first_vectors)
    seconds = (second_attn_in, second_attn_out, second_mlp_in, second_mlp_out, second_vectors)
    settings = ((D ** (-0.5), 0.05), ((D // 8) ** (-0.5), 0.05), (D ** (-0.5), 0.05), (FF ** (-0.5), 0.05), (0.3, 0.0))
    updated = [adamw(params[index], gradients[index + 1], firsts[index], seconds[index], settings[index][0], settings[index][1]) for index in range(5)]
    return (result.astype(jnp.bfloat16), gradients[0], updated[0][0], updated[1][0], updated[2][0], updated[3][0], updated[4][0], updated[0][1], updated[1][1], updated[2][1], updated[3][1], updated[4][1], updated[0][2], updated[1][2], updated[2][2], updated[3][2], updated[4][2])
```

```python
import functools
import math

import jax
import jax.numpy as jnp
from jax import lax
from jax.experimental import pallas as pl
from jax.experimental.pallas import tpu as pltpu
from jax.sharding import PartitionSpec as P

MESH = pl.DeviceIdType.MESH
ALL = slice(None)


class Shape:
    def __init__(self, mesh):
        self.X = mesh.shape["node"] // 2
        chips = mesh.shape["chip"]
        self.Q = 2 ** ((chips.bit_length() - 1) // 2)
        self.P = chips // self.Q
        self.devices = mesh.shape["node"] * chips
        self.grid = (self.X, 2, self.P, self.Q)


class Place(Shape):
    def __init__(self, shape):
        self.__dict__.update(shape.__dict__)
        node, chip = lax.axis_index("node"), lax.axis_index("chip")
        self.x, self.c = node // 2, lax.rem(node, 2)
        self.p, self.q = chip // self.Q, lax.rem(chip, self.Q)

    def size(self, axis):
        return {"x": self.X, "p": self.P, "q": self.Q, "c": 2}[axis]

    def mine(self, axis):
        return {"x": self.x, "p": self.p, "q": self.q, "c": self.c}[axis]

    def off(self, axis, k):
        n = self.size(axis)
        return lax.rem(self.mine(axis) + (k % n), n)

    def device(self, axis, k):
        at = {"x": self.x, "p": self.p, "q": self.q, "c": self.c}
        at[axis] = self.off(axis, k)
        return (at["x"] * 2 + at["c"], at["p"] * self.Q + at["q"])

    def peers(self):
        return [(a, k) for a in ("p", "q", "x", "c") for k in range(1, self.size(a))]

    def greet(self):
        barrier = pltpu.get_barrier_semaphore()
        peers = self.peers()
        for axis, k in peers:
            pl.semaphore_signal(barrier, inc=1, device_id=self.device(axis, k), device_id_type=MESH)
        pl.semaphore_wait(barrier, len(peers))


def gather_copies(shape):
    return (shape.P - 1) + 2 * (shape.X - 1) + 2 * (shape.Q - 1) + 1


class Gather:
    def __init__(self, at, src, dst, cols, order, send, recv, local):
        self.at, self.src, self.dst, self.cols, self.order = at, src, dst, cols, order
        self.send, self.recv, self.local = send, recv, local
        self.used = 0
        self.started = []
        self.arrivals = {}

    def region(self, **fix):
        at = self.at
        pick = dict(x=at.x, p=at.p, q=at.q, c=at.c)
        pick.update(fix)
        return self.dst.at[pick["x"], pick["c"], pick["p"], pick["q"], :, self.cols]

    def push(self, phase, axis, k, held, src=None):
        at, slot = self.at, self.used
        self.used += 1
        out = self.region(**held)
        if axis == "c":
            came = self.region(**dict(held, c=1 - at.c))
        else:
            came = self.region(**dict(held, **{axis: at.off(axis, -k)}))
        sems = dict(send_sem=self.send.at[slot], recv_sem=self.recv.at[slot])
        copy = pltpu.make_async_remote_copy(
            src_ref=out if src is None else src, dst_ref=out, device_id=at.device(axis, k), device_id_type=MESH, **sems)
        copy.start()
        self.started.append(copy)
        arrive = pltpu.make_async_remote_copy(
            src_ref=came, dst_ref=came, device_id=at.device(axis, k), device_id_type=MESH, **sems)
        self.arrivals.setdefault(phase, []).append(arrive)

    def settle(self, phase):
        for copy in self.arrivals.pop(phase, []):
            copy.wait_recv()

    def step(self, phase):
        at = self.at
        second, third = self.order
        if phase == 0:
            own = self.src.at[:, self.cols]
            self.keep = pltpu.make_async_copy(own, self.region(), self.local)
            self.keep.start()
            for k in range(1, at.P):
                self.push(1, "p", k, {}, src=own)
        elif phase == 1:
            self.keep.wait()
            self.settle(1)
            for k in range(1, at.size(second)):
                self.push(2, second, k, dict(p=ALL))
            self.push(4, "c", 1, dict(p=ALL))
        elif phase == 2:
            self.settle(2)
            for k in range(1, at.size(third)):
                self.push(3, third, k, {"p": ALL, second: ALL})
            for k in range(1, at.size(second)):
                self.push(4, "c", 1, {"p": ALL, second: at.off(second, k)})
        elif phase == 3:
            self.settle(3)
            for k in range(1, at.size(third)):
                self.push(4, "c", 1, {"p": ALL, second: ALL, third: at.off(third, k)})
        elif phase == 4:
            self.settle(4)

    def finish(self):
        for copy in self.started:
            copy.wait_send()


def halves(width, parts):
    piece = width // parts
    return [
        (pl.ds(i * piece, piece // 2), pl.ds(i * piece + piece // 2, piece // 2)) for i in range(parts)
    ]


def gather_kernel(shape, parts, *refs):
    n = len(parts)
    srcs, dsts = refs[:n], refs[n : 2 * n]
    send, recv, local = refs[2 * n :]
    at = Place(shape)
    at.greet()
    jobs = []
    for src, dst, count in zip(srcs, dsts, parts):
        for pair in halves(src.shape[1], count):
            jobs.append([])
            for cols, order in zip(pair, (("q", "x"), ("x", "q"))):
                slot = 2 * (len(jobs) - 1) + len(jobs[-1])
                jobs[-1].append(Gather(at, src, dst, cols, order, send.at[slot], recv.at[slot], local.at[slot]))
    for step in range(len(jobs) + 4):
        for phase in range(4, -1, -1):
            if 0 <= step - phase < len(jobs):
                for job in jobs[step - phase]:
                    job.step(phase)
    for pair in jobs:
        for job in pair:
            job.finish()


def all_gather(shape, arrays, parts, collective_id):
    count = 2 * sum(parts)
    copies = gather_copies(shape)
    return pl.pallas_call(
        functools.partial(gather_kernel, shape, parts),
        out_shape=[jax.ShapeDtypeStruct(shape.grid + a.shape, a.dtype) for a in arrays],
        in_specs=[pl.BlockSpec(memory_space=pl.ANY)] * len(arrays),
        out_specs=[pl.BlockSpec(memory_space=pl.ANY)] * len(arrays),
        scratch_shapes=[
            pltpu.SemaphoreType.DMA((count, copies)),
            pltpu.SemaphoreType.DMA((count, copies)),
            pltpu.SemaphoreType.DMA((count,)),
        ],
        compiler_params=pltpu.CompilerParams(
            collective_id=collective_id, has_side_effects=True, vmem_limit_bytes=16 * 2**20),
    )(*arrays)


class Scatter:
    def __init__(self, at, src, out, cols, order, acc, bufs, send, recv, local):
        self.at, self.src, self.out, self.cols, self.order = at, src, out, cols, order
        self.acc, self.bufs, self.send, self.recv, self.local = acc, bufs, send, recv, local
        self.used = 0
        self.started = []
        self.waiting = []

    def part(self, **fix):
        return tuple(fix.get(a, ALL) for a in ("x", "p", "q"))

    def push(self, axis, k, src, dst):
        slot = self.used
        self.used += 1
        copy = pltpu.make_async_remote_copy(
            src_ref=src, dst_ref=dst, send_sem=self.send.at[slot], recv_sem=self.recv.at[slot],
            device_id=self.at.device(axis, k), device_id_type=MESH)
        copy.start()
        self.started.append(copy)
        self.waiting.append(copy)

    def settle(self):
        for copy in self.waiting:
            copy.wait_recv()
        self.waiting = []

    def add(self, index, terms):
        total = self.acc[index]
        for term in terms:
            total = total + term
        self.acc[index] = total

    def step(self, phase):
        at, acc = self.at, self.acc
        first, second = self.order
        b0, b1, b2, b3 = self.bufs
        if phase == 0:
            self.keep = pltpu.make_async_copy(self.src.at[:, at.c, :, :, :, self.cols], acc, self.local)
            self.keep.start()
            self.push("c", 1, self.src.at[:, 1 - at.c, :, :, :, self.cols], b0)
        elif phase == 1:
            self.keep.wait()
            self.settle()
            for i in range(at.X):
                self.add(i, [b0[i]])
            for k in range(1, at.size(first)):
                self.push(first, k, acc.at[self.part(**{first: at.off(first, k)})], b1.at[k - 1])
        elif phase == 2:
            self.settle()
            own = self.part(**{first: at.mine(first)})
            self.add(own, [b1[k - 1] for k in range(1, at.size(first))])
            for k in range(1, at.size(second)):
                self.push(second, k, acc.at[self.part(**{first: at.mine(first), second: at.off(second, k)})], b2.at[k - 1])
        elif phase == 3:
            self.settle()
            own = self.part(x=at.x, q=at.q)
            self.add(own, [b2[k - 1] for k in range(1, at.size(second))])
            for k in range(1, at.P):
                self.push("p", k, acc.at[at.x, at.off("p", k), at.q], b3.at[k - 1])
        elif phase == 4:
            self.settle()
            total = acc[at.x, at.p, at.q].astype(jnp.float32)
            for k in range(1, at.P):
                total = total + b3[k - 1].astype(jnp.float32)
            self.out[:, self.cols] = total

    def finish(self):
        for copy in self.started:
            copy.wait_send()


def scatter_copies(shape):
    return 1 + (shape.X - 1) + (shape.Q - 1) + (shape.P - 1)


def scatter_buffers(shape, rows, width, order):
    X, P, Q = shape.X, shape.P, shape.Q
    block = (rows, width)
    if order[0] == "x":
        first = (X - 1, P, Q) + block
        second = (Q - 1, P) + block
    else:
        first = (Q - 1, X, P) + block
        second = (X - 1, P) + block
    return [(X, P, Q) + block, (X, P, Q) + block, first, second, (P - 1,) + block]


ORDERS = (("x", "q"), ("q", "x"))


def scatter_kernel(shape, parts, *refs):
    n = len(parts)
    srcs, outs = refs[:n], refs[n : 2 * n]
    count = 2 * sum(parts)
    bufs = refs[2 * n : 2 * n + 5 * count]
    send, recv, local = refs[2 * n + 5 * count :]
    at = Place(shape)
    at.greet()
    jobs = []
    for src, out, pieces in zip(srcs, outs, parts):
        for pair in halves(src.shape[-1], pieces):
            jobs.append([])
            for cols, order in zip(pair, ORDERS):
                slot = 2 * (len(jobs) - 1) + len(jobs[-1])
                mine = bufs[5 * slot : 5 * slot + 5]
                jobs[-1].append(
                    Scatter(at, src, out, cols, order, mine[0], mine[1:], send.at[slot], recv.at[slot], local.at[slot]))
    for step in range(len(jobs) + 4):
        for phase in range(4, -1, -1):
            if 0 <= step - phase < len(jobs):
                for job in jobs[step - phase]:
                    job.step(phase)
    for pair in jobs:
        for job in pair:
            job.finish()


def reduce_scatter(shape, arrays, parts, collective_id):
    count, copies = 2 * sum(parts), scatter_copies(shape)
    scratch = []
    for a, pieces in zip(arrays, parts):
        rows, cols = a.shape[-2:]
        for _ in range(pieces):
            for order in ORDERS:
                scratch += [
                    pltpu.VMEM(s, jnp.bfloat16) for s in scatter_buffers(shape, rows, cols // pieces // 2, order)
                ]
    return pl.pallas_call(
        functools.partial(scatter_kernel, shape, parts),
        out_shape=[jax.ShapeDtypeStruct(a.shape[-2:], jnp.float32) for a in arrays],
        in_specs=[pl.BlockSpec(memory_space=pl.ANY)] * len(arrays),
        out_specs=[pl.BlockSpec(memory_space=pltpu.VMEM)] * len(arrays),
        scratch_shapes=scratch
        + [
            pltpu.SemaphoreType.DMA((count, copies)),
            pltpu.SemaphoreType.DMA((count, copies)),
            pltpu.SemaphoreType.DMA((count,)),
        ],
        compiler_params=pltpu.CompilerParams(
            collective_id=collective_id, has_side_effects=True, vmem_limit_bytes=60 * 2**20),
    )(*arrays)

GATHER_PARTS = (3, 1, 2, 2)
SCATTER_PARTS = (3, 1, 4, 4)
SLAB = (16, 256)


def pack_vectors(mine):
    flat = mine.reshape(-1)
    return jnp.pad(flat, (0, SLAB[0] * SLAB[1] - flat.size)).reshape(SLAB)


def unpack_vectors(slabs, layers, entries):
    flat = slabs.reshape(-1, SLAB[0] * SLAB[1])[:, : layers * entries]
    return flat.reshape(-1, layers, entries).transpose(1, 0, 2).reshape(layers, -1)


def spread_vectors(shape, terms):
    layers, entries = terms.shape
    flat = terms.reshape(layers, shape.devices, -1).transpose(1, 0, 2).reshape(shape.devices, -1)
    flat = jnp.pad(flat, ((0, 0), (0, SLAB[0] * SLAB[1] - flat.shape[1])))
    return flat.reshape(shape.grid + SLAB)


D = 1024
HEADS = 16
HEAD_DIM = 64
FF = 4096
STEP = 10
SEQ = 145


norm_eps = 1e-06
beta_first = 0.9
beta_second = 0.999
adam_eps = 1e-08


def norm_forward(values, gain_row, shift_row):
    centre = jnp.mean(values, axis=-1, keepdims=True)
    centred = values - centre
    spread = jnp.mean(centred * centred, axis=-1, keepdims=True)
    inverse = lax.rsqrt(spread + norm_eps)
    normal = centred * inverse
    return (normal * gain_row + shift_row, normal, inverse)


def norm_backward(upstream, normal, inverse, gain_row):
    d_gain = jnp.sum(upstream * normal, axis=0)
    d_shift = jnp.sum(upstream, axis=0)
    scaled = upstream * gain_row
    inner = (
        scaled
        - jnp.mean(scaled, axis=-1, keepdims=True)
        - normal * jnp.mean(scaled * normal, axis=-1, keepdims=True)
    )
    return (inverse * inner, d_gain, d_shift)


def split_vector(vector_row):
    pieces = [vector_row[index * D : (index + 1) * D] for index in range(10)]
    return pieces + [vector_row[10 * D :]]


def attend_scores(query_b, key_b):
    return jnp.einsum(
        "gqhc,gkhc->ghqk", query_b, key_b, preferred_element_type=jnp.float32
    ) * HEAD_DIM ** (-0.5)


def forward_layer(hidden, matrices, vector_row):
    w_in, w_out, w_up, w_down = matrices
    gain_a, shift_a, bias_q, bias_v, bias_o, scale_a, gain_m, shift_m, bias_d, scale_m, bias_u = (
        split_vector(vector_row)
    )
    images = hidden.shape[0] // SEQ
    heads_shape = (images, SEQ, HEADS, HEAD_DIM)
    normed_a, normal_a, inverse_a = norm_forward(hidden, gain_a, shift_a)
    normed_a_b = normed_a.astype(jnp.bfloat16)
    projected = jnp.dot(normed_a_b, w_in, preferred_element_type=jnp.float32)
    projected = projected + jnp.concatenate([bias_q, jnp.zeros_like(bias_q), bias_v])
    query_b = projected[:, :D].astype(jnp.bfloat16).reshape(heads_shape)
    key_b = projected[:, D : 2 * D].astype(jnp.bfloat16).reshape(heads_shape)
    value_b = projected[:, 2 * D :].astype(jnp.bfloat16).reshape(heads_shape)
    scores = attend_scores(query_b, key_b)
    top_score = jnp.max(scores, axis=-1, keepdims=True)
    expo = jnp.exp(scores - top_score)
    total = jnp.sum(expo, axis=-1, keepdims=True)
    probs_b = (expo / total).astype(jnp.bfloat16)
    log_total = top_score + jnp.log(total)
    mixed = jnp.einsum("ghqk,gkhc->gqhc", probs_b, value_b, preferred_element_type=jnp.float32)
    mixed_b = mixed.reshape(-1, D).astype(jnp.bfloat16)
    branch = jnp.dot(mixed_b, w_out, preferred_element_type=jnp.float32) + bias_o
    middle = hidden + scale_a * branch
    normed_m, normal_m, inverse_m = norm_forward(middle, gain_m, shift_m)
    normed_m_b = normed_m.astype(jnp.bfloat16)
    upper = jnp.dot(normed_m_b, w_up, preferred_element_type=jnp.float32) + bias_u
    active_b = jax.nn.gelu(upper, approximate=False).astype(jnp.bfloat16)
    down = jnp.dot(active_b, w_down, preferred_element_type=jnp.float32) + bias_d
    result = middle + scale_m * down
    saved = (
        normal_a,
        inverse_a,
        normed_a_b,
        query_b,
        key_b,
        value_b,
        log_total,
        mixed_b,
        branch,
        normal_m,
        inverse_m,
        normed_m_b,
        upper,
        active_b,
        down,
    )
    return (result, saved)


def backward_layer(upstream, saved, matrices, vector_row):
    w_in, w_out, w_up, w_down = matrices
    gain_a, shift_a, bias_q, bias_v, bias_o, scale_a, gain_m, shift_m, bias_d, scale_m, bias_u = (
        split_vector(vector_row)
    )
    (
        normal_a,
        inverse_a,
        normed_a_b,
        query_b,
        key_b,
        value_b,
        log_total,
        mixed_b,
        branch,
        normal_m,
        inverse_m,
        normed_m_b,
        upper,
        active_b,
        down,
    ) = saved
    d_scale_m = jnp.sum(upstream * down, axis=0)
    d_down = upstream * scale_m
    d_bias_d = jnp.sum(d_down, axis=0)
    d_down_b = d_down.astype(jnp.bfloat16)
    g_down = jnp.einsum("tf,td->fd", active_b, d_down_b, preferred_element_type=jnp.float32)
    d_active = jnp.einsum("td,fd->tf", d_down_b, w_down, preferred_element_type=jnp.float32)
    cumulative = 0.5 * (1.0 + lax.erf(upper * 0.5**0.5))
    density = jnp.exp(-0.5 * upper * upper) * (2.0 * math.pi) ** (-0.5)
    d_upper = d_active * (cumulative + upper * density)
    d_bias_u = jnp.sum(d_upper, axis=0)
    d_upper_b = d_upper.astype(jnp.bfloat16)
    g_up = jnp.einsum("td,tf->df", normed_m_b, d_upper_b, preferred_element_type=jnp.float32)
    d_normed_m = jnp.einsum("tf,df->td", d_upper_b, w_up, preferred_element_type=jnp.float32)
    d_middle, d_gain_m, d_shift_m = norm_backward(d_normed_m, normal_m, inverse_m, gain_m)
    d_middle = d_middle + upstream
    d_scale_a = jnp.sum(d_middle * branch, axis=0)
    d_branch = d_middle * scale_a
    d_bias_o = jnp.sum(d_branch, axis=0)
    d_branch_b = d_branch.astype(jnp.bfloat16)
    g_out = jnp.einsum("td,te->de", mixed_b, d_branch_b, preferred_element_type=jnp.float32)
    d_mixed_b = jnp.einsum(
        "te,de->td", d_branch_b, w_out, preferred_element_type=jnp.float32
    ).astype(jnp.bfloat16)
    d_mixed_b = d_mixed_b.reshape(query_b.shape)
    scores = attend_scores(query_b, key_b)
    probs = jnp.exp(scores - log_total)
    probs_b = probs.astype(jnp.bfloat16)
    d_probs = jnp.einsum("gqhc,gkhc->ghqk", d_mixed_b, value_b, preferred_element_type=jnp.float32)
    d_value = jnp.einsum("ghqk,gqhc->gkhc", probs_b, d_mixed_b, preferred_element_type=jnp.float32)
    d_scores = probs * (d_probs - jnp.sum(probs * d_probs, axis=-1, keepdims=True))
    d_scores_b = d_scores.astype(jnp.bfloat16)
    d_query = jnp.einsum(
        "ghqk,gkhc->gqhc", d_scores_b, key_b, preferred_element_type=jnp.float32
    ) * HEAD_DIM ** (-0.5)
    d_key = jnp.einsum(
        "ghqk,gqhc->gkhc", d_scores_b, query_b, preferred_element_type=jnp.float32
    ) * HEAD_DIM ** (-0.5)
    rows = upstream.shape[0]
    d_query = d_query.reshape(rows, D)
    d_value = d_value.reshape(rows, D)
    d_projected = jnp.concatenate([d_query, d_key.reshape(rows, D), d_value], axis=1)
    d_bias_q = jnp.sum(d_query, axis=0)
    d_bias_v = jnp.sum(d_value, axis=0)
    d_projected_b = d_projected.astype(jnp.bfloat16)
    g_in = jnp.einsum("td,te->de", normed_a_b, d_projected_b, preferred_element_type=jnp.float32)
    d_normed_a = jnp.einsum("te,de->td", d_projected_b, w_in, preferred_element_type=jnp.float32)
    d_hidden, d_gain_a, d_shift_a = norm_backward(d_normed_a, normal_a, inverse_a, gain_a)
    d_hidden = d_hidden + d_middle
    d_vector = jnp.concatenate(
        [
            d_gain_a,
            d_shift_a,
            d_bias_q,
            d_bias_v,
            d_bias_o,
            d_scale_a,
            d_gain_m,
            d_shift_m,
            d_bias_d,
            d_scale_m,
            d_bias_u,
        ]
    )
    return (d_hidden, (g_in, g_out, g_up, g_down, d_vector))


def adamw(weight, gradient, first, second, rate, decay):
    first_new = beta_first * first + (1.0 - beta_first) * gradient
    second_new = beta_second * second + (1.0 - beta_second) * gradient * gradient
    fix_first = 1.0 - beta_first**STEP
    fix_second = 1.0 - beta_second**STEP
    stepped = first_new / fix_first / (jnp.sqrt(second_new / fix_second) + adam_eps)
    return (weight - rate * (stepped + decay * weight), first_new, second_new)


def on_device(
    shape,
    tokens,
    cotangent,
    w_attn_in,
    w_attn_out,
    w_mlp_in,
    w_mlp_out,
    vectors,
    first_attn_in,
    first_attn_out,
    first_mlp_in,
    first_mlp_out,
    first_vectors,
    second_attn_in,
    second_attn_out,
    second_mlp_in,
    second_mlp_out,
    second_vectors,
):
    shards = (w_attn_in, w_attn_out, w_mlp_in, w_mlp_out, vectors)
    layers = w_attn_in.shape[0]
    token_rows = tokens.shape[0] * tokens.shape[1]
    blocks = [shards[m][l].astype(jnp.bfloat16) for l in range(layers) for m in range(4)]
    packed = pack_vectors(vectors.astype(jnp.bfloat16))
    gathered = all_gather(shape, [packed] + blocks, (1,) + GATHER_PARTS * layers, 1)
    vector_rows = unpack_vectors(gathered[0], layers, vectors.shape[1]).astype(jnp.float32)
    weights = [
        [w.reshape(-1, w.shape[-1]) for w in gathered[1 + 4 * l : 5 + 4 * l]] for l in range(layers)
    ]
    hidden = tokens.astype(jnp.float32).reshape(token_rows, D)
    kept_values = []
    for layer_index in range(layers):
        hidden, saved = forward_layer(hidden, weights[layer_index], vector_rows[layer_index])
        kept_values.append(saved)
    output = hidden.reshape(tokens.shape).astype(jnp.bfloat16)
    upstream = cotangent.astype(jnp.float32).reshape(token_rows, D)
    collected = [None] * layers
    vector_terms = [None] * layers
    for layer_index in reversed(range(layers)):
        upstream, terms = backward_layer(
            upstream, kept_values[layer_index], weights[layer_index], vector_rows[layer_index]
        )
        vector_terms[layer_index] = terms[4]
        blocks = [
            t.astype(jnp.bfloat16).reshape(shape.grid + (t.shape[0] // shape.devices, t.shape[1])) for t in terms[:4]
        ]
        parts = SCATTER_PARTS
        if layer_index == 0:
            blocks = blocks + [spread_vectors(shape, jnp.stack(vector_terms).astype(jnp.bfloat16))]
            parts = parts + (1,)
        collected[layer_index] = reduce_scatter(shape, blocks, parts, 2 + layer_index)
    stacked = [jnp.stack([collected[l][member] for l in range(layers)]) for member in range(4)]
    stacked.append(collected[0][4].reshape(-1)[: vectors.size].reshape(vectors.shape))
    firsts = (first_attn_in, first_attn_out, first_mlp_in, first_mlp_out, first_vectors)
    seconds = (second_attn_in, second_attn_out, second_mlp_in, second_mlp_out, second_vectors)
    settings = (
        (D ** (-0.5), 0.05),
        ((D // 8) ** (-0.5), 0.05),
        (D ** (-0.5), 0.05),
        (FF ** (-0.5), 0.05),
        (0.3, 0.0),
    )
    updated = [
        adamw(
            shards[member],
            stacked[member],
            firsts[member],
            seconds[member],
            settings[member][0],
            settings[member][1],
        )
        for member in range(5)
    ]
    d_tokens = upstream.reshape(tokens.shape)
    return (
        output,
        d_tokens,
        updated[0][0],
        updated[1][0],
        updated[2][0],
        updated[3][0],
        updated[4][0],
        updated[0][1],
        updated[1][1],
        updated[2][1],
        updated[3][1],
        updated[4][1],
        updated[0][2],
        updated[1][2],
        updated[2][2],
        updated[3][2],
        updated[4][2],
    )


def solution(mesh):
    in_specs = (
        P(("node", "chip"), None, None),
        P(("node", "chip"), None, None),
        P(None, ("node", "chip"), None),
        P(None, ("node", "chip"), None),
        P(None, ("node", "chip"), None),
        P(None, ("node", "chip"), None),
        P(None, ("node", "chip")),
        P(None, ("node", "chip"), None),
        P(None, ("node", "chip"), None),
        P(None, ("node", "chip"), None),
        P(None, ("node", "chip"), None),
        P(None, ("node", "chip")),
        P(None, ("node", "chip"), None),
        P(None, ("node", "chip"), None),
        P(None, ("node", "chip"), None),
        P(None, ("node", "chip"), None),
        P(None, ("node", "chip")),
    )
    out_specs = (
        P(("node", "chip"), None, None),
        P(("node", "chip"), None, None),
        P(None, ("node", "chip"), None),
        P(None, ("node", "chip"), None),
        P(None, ("node", "chip"), None),
        P(None, ("node", "chip"), None),
        P(None, ("node", "chip")),
        P(None, ("node", "chip"), None),
        P(None, ("node", "chip"), None),
        P(None, ("node", "chip"), None),
        P(None, ("node", "chip"), None),
        P(None, ("node", "chip")),
        P(None, ("node", "chip"), None),
        P(None, ("node", "chip"), None),
        P(None, ("node", "chip"), None),
        P(None, ("node", "chip"), None),
        P(None, ("node", "chip")),
    )
    return jax.shard_map(
        functools.partial(on_device, Shape(mesh)), mesh=mesh, in_specs=in_specs, out_specs=out_specs, check_vma=False
    )
```

```python
import functools
import math

import jax
import jax.numpy as jnp
from jax import lax
from jax.experimental import pallas as pl
from jax.experimental.pallas import tpu as pltpu
from jax.sharding import PartitionSpec as P

STEP = 10
beta_first = 0.9
beta_second = 0.999
adam_eps = 1e-08
SLAB = (16, 256)
MESH = pl.DeviceIdType.MESH
ALL = slice(None)
D = 1024
HEADS = 16
HEAD_DIM = 64
FF = 4096
SEQ = 145
SPAN = 160
GROUP = 256
FF_TILE = 512
ROWS = 16
norm_eps = 1e-06
LOW = jnp.bfloat16
FULL = jnp.float32
GAIN_A, SHIFT_A, BIAS_Q, BIAS_V, BIAS_O, SCALE_A, GAIN_M, SHIFT_M, BIAS_D, SCALE_M, BIAS_U = range(11)


class Shape:
    def __init__(self, mesh):
        chips = mesh.shape["chip"]
        self.X = mesh.shape["node"] // 2
        self.Q = 2 ** ((chips.bit_length() - 1) // 2)
        self.P = chips // self.Q
        self.devices = mesh.shape["node"] * chips
        self.grid = (self.X, 2, self.P, self.Q)
        self.sizes = {"x": self.X, "c": 2, "p": self.P, "q": self.Q}


class Place:
    def __init__(self, shape):
        self.sizes = shape.sizes
        node, chip = lax.axis_index("node"), lax.axis_index("chip")
        self.at = {"x": node // 2, "c": lax.rem(node, 2), "p": chip // shape.Q, "q": lax.rem(chip, shape.Q)}
        self.offs, self.devices = {}, {}
        for axis, n in shape.sizes.items():
            for k in range(1, n):
                off = lax.rem(self.at[axis] + k, n)
                to = dict(self.at, **{axis: off})
                self.offs[axis, k] = off
                self.devices[axis, k] = (to["x"] * 2 + to["c"], to["p"] * shape.Q + to["q"])

    def off(self, axis, k):
        return self.offs[axis, k % self.sizes[axis]]

    def greet(self):
        barrier = pltpu.get_barrier_semaphore()
        for device in self.devices.values():
            pl.semaphore_signal(barrier, inc=1, device_id=device, device_id_type=MESH)
        pl.semaphore_wait(barrier, len(self.devices))


class Move:
    def __init__(self, src, dst, came, sems, device):
        if device is None:
            copy = functools.partial(pltpu.make_async_copy, src, dst, sems[0])
            self.start, self.arrived, self.sent = lambda: copy().start(), lambda: copy().wait(), None
        else:
            copy = functools.partial(
                pltpu.make_async_remote_copy,
                send_sem=sems[0], recv_sem=sems[1], device_id=device, device_id_type=MESH)
            self.start = lambda: copy(src, dst).start()
            self.sent = lambda: copy(src, dst).wait_send()
            self.arrived = lambda: copy(came, came).wait_recv()


class Task:
    def __init__(self, place, sems):
        self.place, self.sems, self.used = place, sems, 0
        self.phases = [([], [], []) for _ in range(5)]

    def move(self, begin, end, src, dst, came=None, axis=None, k=None):
        slot, self.used = self.used, self.used + 1
        sems = (self.sems[0].at[slot], self.sems[1].at[slot])
        move = Move(src, dst, dst if came is None else came, sems, None if axis is None else self.place.devices[axis, k])
        self.phases[begin][2].append(move)
        self.phases[end][0].append(move)


class Pipeline:
    def __init__(self, place, jobs):
        self.place, self.jobs = place, jobs

    def plan(self, steps):
        flying, unsent, todo = [], [], {}
        for step in steps:
            acts = todo[step] = []
            for phase in range(4, -1, -1):
                if not 0 <= step - phase < len(self.jobs):
                    continue
                for task in self.jobs[step - phase]:
                    waits, work, starts = task.phases[phase]
                    acts += [move.arrived for move in waits if move in flying]
                    flying = [move for move in flying if move not in waits] + starts
                    acts += work + [move.start for move in starts]
                    unsent += [move.sent for move in starts if move.sent is not None]
        return todo, [move.arrived for move in flying] + unsent


class Gather(Task):
    def __init__(self, place, src, dst, cols, order, sems):
        super().__init__(place, sems)
        at, sizes = place.at, place.sizes
        second, third = order

        def region(**fix):
            pick = dict(at, **fix)
            return dst.at[pick["x"], pick["c"], pick["p"], pick["q"], :, cols]

        def push(begin, end, axis, k, own=None, **held):
            came = region(**dict(held, **{axis: place.off(axis, -k)}))
            self.move(begin, end, region(**held) if own is None else own, region(**held), came, axis, k)

        if src is not None:
            own = src.at[:, cols]
            self.move(0, 1, own, region())
            for k in range(1, sizes["p"]):
                push(0, 1, "p", k, own)
        for k in range(1, sizes[second]):
            push(1, 2, second, k, p=ALL)
        push(1, 4, "c", 1, p=ALL)
        for k in range(1, sizes[third]):
            push(2, 3, third, k, **{"p": ALL, second: ALL})
        for k in range(1, sizes[second]):
            push(2, 4, "c", 1, **{"p": ALL, second: place.off(second, k)})
        for k in range(1, sizes[third]):
            push(3, 4, "c", 1, **{"p": ALL, second: ALL, third: place.off(third, k)})


class Scatter(Task):
    def __init__(self, place, src, out, cols, order, bufs, sems):
        super().__init__(place, sems)
        at, sizes = place.at, place.sizes
        first, second = order
        acc, b0, b1, b2, b3 = bufs

        def part(**fix):
            return tuple(fix.get(a, ALL) for a in ("x", "p", "q"))

        def add(index, terms):
            total = acc[index]
            for term in terms:
                total = total + term[...]
            acc[index] = total

        def finish():
            total = acc[at["x"], at["p"], at["q"]].astype(FULL)
            for k in range(1, sizes["p"]):
                total = total + b3[k - 1].astype(FULL)
            out[:, cols] = total

        self.move(0, 1, src.at[:, at["c"], :, :, :, cols], acc)
        self.move(0, 1, src.at[:, place.off("c", 1), :, :, :, cols], b0, None, "c", 1)
        for i in range(sizes["x"]):
            self.phases[1][1].append(functools.partial(add, i, [b0.at[i]]))
        for k in range(1, sizes[first]):
            self.move(1, 2, acc.at[part(**{first: place.off(first, k)})], b1.at[k - 1], None, first, k)
        self.phases[2][1].append(
            functools.partial(add, part(**{first: at[first]}), [b1.at[k - 1] for k in range(1, sizes[first])]))
        for k in range(1, sizes[second]):
            away = part(**{first: at[first], second: place.off(second, k)})
            self.move(2, 3, acc.at[away], b2.at[k - 1], None, second, k)
        self.phases[3][1].append(
            functools.partial(add, part(x=at["x"], q=at["q"]), [b2.at[k - 1] for k in range(1, sizes[second])]))
        for k in range(1, sizes["p"]):
            self.move(3, 4, acc.at[at["x"], place.off("p", k), at["q"]], b3.at[k - 1], None, "p", k)
        self.phases[4][1].append(finish)


def halves(width, piece, pieces):
    size = width // pieces // 2
    return [pl.ds((2 * piece + i) * size, size) for i in range(2)]


ANYWHERE = pl.BlockSpec(memory_space=pl.ANY)


class Gathering:
    def __init__(self, shape, sources, jobs, first, last, held):
        self.shape, self.jobs, self.steps, self.held = shape, jobs, list(range(first, last)), held
        active = [i for i in range(len(jobs)) if i < last and i + 4 >= first]
        self.active = active
        self.fresh = sorted({m for i in active if i >= first for m, _, _ in jobs[i]})
        self.names = sorted({m for i in active for m, _, _ in jobs[i]})
        under_way = [m for m in self.names if m in held]
        self.inputs = [sources[m] for m in self.fresh] + [held[m] for m in under_way]
        self.in_specs = [ANYWHERE] * len(self.inputs)
        self.out_shape = [jax.ShapeDtypeStruct(shape.grid + sources[m].shape, LOW) for m in self.names]
        self.out_specs = [ANYWHERE] * len(self.names)
        self.aliases = {len(self.fresh) + i: self.names.index(m) for i, m in enumerate(under_way)}
        tasks = sum(2 * len(jobs[i]) for i in active)
        sizes = shape.sizes
        copies = sizes["p"] + 2 * (sizes["x"] - 1) + 2 * (sizes["q"] - 1) + 1
        self.scratch = [pltpu.SemaphoreType.DMA((tasks, copies))] * 2

    def build(self, ins, outs, scratch):
        place = Place(self.shape)
        send, recv = scratch
        made, slot = [], 0
        for i, job in enumerate(self.jobs):
            made.append([])
            if i not in self.active:
                continue
            for name, piece, pieces in job:
                dst = outs[self.names.index(name)]
                src = ins[self.fresh.index(name)] if i >= self.steps[0] else None
                for cols, order in zip(halves(dst.shape[-1], piece, pieces), (("q", "x"), ("x", "q"))):
                    made[-1].append(Gather(place, src, dst, cols, order, (send.at[slot], recv.at[slot])))
                    slot += 1
        return Pipeline(place, made)

    def take(self, outs):
        self.held.update(zip(self.names, outs))


class Scattering:
    def __init__(self, shape, arrays, pieces):
        self.shape, self.pieces = shape, pieces
        self.inputs, self.in_specs = list(arrays), [ANYWHERE] * len(arrays)
        self.steps = list(range(sum(pieces) + 4))
        self.out_shape = [jax.ShapeDtypeStruct(a.shape[-2:], FULL) for a in arrays]
        self.out_specs = [whole(a.shape[-2:]) for a in arrays]
        self.aliases = {}
        X, P_, Q = shape.X, shape.P, shape.Q
        self.scratch = []
        for a, n in zip(arrays, pieces):
            block = (a.shape[-2], a.shape[-1] // n // 2)
            for _ in range(n):
                for one in (((X - 1, P_, Q), (Q - 1, P_)), ((Q - 1, X, P_), (X - 1, P_))):
                    for lead in ((X, P_, Q), (X, P_, Q)) + one + ((P_ - 1,),):
                        self.scratch.append(pltpu.VMEM(lead + block, LOW))
        tasks = 2 * sum(pieces)
        copies = 2 + (X - 1) + (Q - 1) + (P_ - 1)
        self.scratch += [pltpu.SemaphoreType.DMA((tasks, copies))] * 2

    def build(self, ins, outs, scratch):
        place = Place(self.shape)
        send, recv = scratch[-2:]
        made, slot = [], 0
        for src, out, n in zip(ins, outs, self.pieces):
            for piece in range(n):
                made.append([])
                for cols, order in zip(halves(src.shape[-1], piece, n), (("x", "q"), ("q", "x"))):
                    bufs = scratch[5 * slot : 5 * slot + 5]
                    made[-1].append(Scatter(place, src, out, cols, order, bufs, (send.at[slot], recv.at[slot])))
                    slot += 1
        return Pipeline(place, made)

    def take(self, outs):
        self.sums = outs


def beside(kernel, points, transfer, pace, number, grid, inputs, in_specs, out_specs, out_shape, scratch, name, limit=60):
    total = grid * points
    when = {}
    if transfer is not None:
        for i, step in enumerate(transfer.steps):
            when.setdefault(min(total, i * total // pace), []).append(step)
    counts = [len(inputs), len(transfer.inputs) if transfer else 0, len(out_shape), len(transfer.out_shape) if transfer else 0, len(scratch)]

    def body(*refs):
        groups, i = [], 0
        for n in counts:
            groups.append(refs[i : i + n])
            i += n
        groups.append(refs[i:])
        step = pl.program_id(0)
        if transfer is None:
            kernel(lambda point: None, *groups[0], *groups[2], *groups[4])
            return
        pipe = transfer.build(groups[1], groups[3], groups[5])
        todo, rest = pipe.plan(transfer.steps)

        def tick(point):
            for time in sorted(when):
                if time < total and time % points == point:
                    @pl.when(step == time // points)
                    def _():
                        if time == 0:
                            pipe.place.greet()
                        for act in [act for s in when[time] for act in todo[s]]:
                            act()

        kernel(tick, *groups[0], *groups[2], *groups[4])

        @pl.when(step == grid - 1)
        def _():
            for act in [act for s in when.get(total, []) for act in todo[s]] + rest:
                act()

    extra = {}
    if transfer is not None:
        extra["input_output_aliases"] = {counts[0] + i: counts[2] + o for i, o in transfer.aliases.items()}
        inputs, in_specs = list(inputs) + transfer.inputs, list(in_specs) + transfer.in_specs
        out_specs, out_shape = list(out_specs) + transfer.out_specs, list(out_shape) + transfer.out_shape
        scratch = list(scratch) + transfer.scratch
    outs = pl.pallas_call(
        body,
        grid=(grid,),
        in_specs=in_specs,
        out_specs=out_specs,
        out_shape=out_shape,
        scratch_shapes=scratch,
        name=name,
        compiler_params=pltpu.CompilerParams(
            dimension_semantics=("arbitrary",),
            vmem_limit_bytes=limit * 2**20,
            collective_id=None if transfer is None else number,
            has_side_effects=transfer is not None,
        ),
        **extra,
    )(*inputs)
    if transfer is not None:
        transfer.take(outs[counts[2] :])
    return outs[: counts[2]]


def mul(a, b):
    return jnp.dot(a, b, preferred_element_type=FULL)


def mul_nt(a, b):
    return lax.dot_general(a, b, (((1,), (1,)), ((), ())), preferred_element_type=FULL)


def mul_tn(a, b):
    return lax.dot_general(a, b, (((0,), (0,)), ((), ())), preferred_element_type=FULL)


def normalise(values):
    centred = values - jnp.mean(values, axis=-1, keepdims=True)
    inverse = lax.rsqrt(jnp.mean(centred * centred, axis=-1, keepdims=True) + norm_eps)
    return centred * inverse, inverse


def tiles(rows, step=160):
    return [slice(i, i + step) for i in range(0, rows, step)]


def row(vec, index):
    return vec[index : index + 1, :]


def softmax_of(q, k, lanes, width):
    scores = mul_nt(jnp.where(lanes, q, jnp.zeros_like(q)), k) * HEAD_DIM ** (-0.5)
    scores = jnp.where(width, scores, -1e30)
    expo = jnp.exp(scores - jnp.max(scores, axis=-1, keepdims=True))
    return expo * (1.0 / jnp.sum(expo, axis=-1, keepdims=True))


def lane_sets():
    lane = lax.broadcasted_iota(jnp.int32, (SPAN, 128), 1)
    return [lane < HEAD_DIM, lane >= HEAD_DIM]


def key_set():
    return lax.broadcasted_iota(jnp.int32, (SPAN, SPAN), 1) < SEQ


def attend_fwd(tick, h, vec, wq, wk, wv, wo, a_out, q_out, k_out, v_out, mixed_out, branch_out, mid_out, mixed, total):
    step, last = pl.program_id(0), pl.num_programs(0) - 1
    rows = h.shape[0]
    tick(0)

    @pl.when(step == 0)
    def _():
        for t in tiles(rows):
            normal, _ = normalise(h[t, :])
            a_out[t, :] = (normal * row(vec, GAIN_A) + row(vec, SHIFT_A)).astype(LOW)
        total[...] = jnp.zeros_like(total)

    group = pl.ds(pl.multiple_of(step * GROUP, GROUP), GROUP)
    q_out[...] = (mul(a_out[...], wq[...]) + vec[BIAS_Q : BIAS_Q + 1, group]).astype(LOW)
    k_out[...] = mul(a_out[...], wk[...]).astype(LOW)
    v_out[...] = (mul(a_out[...], wv[...]) + vec[BIAS_V : BIAS_V + 1, group]).astype(LOW)
    tick(1)
    lanes, width = lane_sets(), key_set()

    def image(i, carry):
        at = pl.ds(pl.multiple_of(i * SPAN, SPAN), SPAN)
        for pair in range(GROUP // 128):
            cols = slice(pair * 128, pair * 128 + 128)
            q, k, v = q_out[at, cols], k_out[at, cols], v_out[at, cols]
            both = [mul(softmax_of(q, k, lanes[s], width).astype(LOW), v) for s in range(2)]
            mixed[at, cols] = jnp.where(lanes[0], both[0], both[1]).astype(LOW)
        return carry

    images = rows // SPAN
    lax.fori_loop(0, images // 2, image, 0)
    tick(2)
    lax.fori_loop(images // 2, images, image, 0)
    mixed_out[...] = mixed[...]
    total[...] += mul(mixed[...], wo[...])

    @pl.when(step == last)
    def _():
        for t in tiles(rows):
            branch = total[t, :] + row(vec, BIAS_O)
            branch_out[t, :] = branch
            mid_out[t, :] = h[t, :] + row(vec, SCALE_A) * branch


def whole(shape):
    return pl.BlockSpec(shape, lambda j: (0,) * len(shape), pipeline_mode=pl.Buffered(1))


def columns(rows, width, at=0):
    return pl.BlockSpec((rows, width), lambda j: (0, j + at))


def lines(height, cols):
    return pl.BlockSpec((height, cols), lambda j: (j, 0))


def attention_forward(h, vec, w_in, w_out, transfer=None, pace=1, number=0):
    rows = h.shape[0]
    n = D // GROUP
    f32, low = lambda s: jax.ShapeDtypeStruct(s, FULL), lambda s: jax.ShapeDtypeStruct(s, LOW)
    full = whole((rows, D))
    cols = columns(rows, GROUP)
    return beside(
        attend_fwd,
        points=3,
        transfer=transfer,
        pace=pace,
        number=number,
        grid=n,
        inputs=[h, vec, w_in, w_in, w_in, w_out],
        in_specs=[full, whole(vec.shape)]
        + [columns(D, GROUP, i * n) for i in range(3)]
        + [lines(GROUP, D)],
        out_specs=[full, cols, cols, cols, cols, full, full],
        out_shape=[low((rows, D))] * 5 + [f32((rows, D))] * 2,
        scratch=[pltpu.VMEM((rows, GROUP), LOW), pltpu.VMEM((rows, D), FULL)],
        name="attention_forward",
    )


def phi_of(u):
    return 0.5 * (1.0 + lax.erf(u * 0.5**0.5))


def mlp_fwd(tick, mid, vec, wu, wd, c_out, u_out, act_out, down_out, next_out, low_out, total):
    step, last = pl.program_id(0), pl.num_programs(0) - 1
    rows = mid.shape[0]
    tick(0)

    @pl.when(step == 0)
    def _():
        for t in tiles(rows):
            normal, _ = normalise(mid[t, :])
            c_out[t, :] = (normal * row(vec, GAIN_M) + row(vec, SHIFT_M)).astype(LOW)
        total[...] = jnp.zeros_like(total)

    per = D // FF_TILE
    bias = vec[pl.ds(BIAS_U + step // per, 1), pl.ds(pl.multiple_of(lax.rem(step, per) * FF_TILE, FF_TILE), FF_TILE)]

    def part(i, carry):
        t = pl.ds(pl.multiple_of(i * SPAN, SPAN), SPAN)
        u = mul(c_out[t, :], wu[...]) + bias
        u_out[t, :] = u
        act = (u * phi_of(u)).astype(LOW)
        act_out[t, :] = act
        total[t, :] += mul(act, wd[...])
        return carry

    images = rows // SPAN
    lax.fori_loop(0, images // 2, part, 0)
    tick(1)
    lax.fori_loop(images // 2, images, part, 0)

    @pl.when(step == last)
    def _():
        for t in tiles(rows):
            down = total[t, :] + row(vec, BIAS_D)
            down_out[t, :] = down
            result = mid[t, :] + row(vec, SCALE_M) * down
            next_out[t, :] = result
            low_out[t, :] = result.astype(LOW)


def mlp_forward(mid, vec, w_up, w_down, transfer=None, pace=1, number=0):
    rows = mid.shape[0]
    f32, low = lambda s: jax.ShapeDtypeStruct(s, FULL), lambda s: jax.ShapeDtypeStruct(s, LOW)
    full = whole((rows, D))
    tile = columns(rows, FF_TILE)
    return beside(
        mlp_fwd,
        points=2,
        transfer=transfer,
        pace=pace,
        number=number,
        grid=FF // FF_TILE,
        inputs=[mid, vec, w_up, w_down],
        in_specs=[full, whole(vec.shape), columns(D, FF_TILE), lines(FF_TILE, D)],
        out_specs=[full, tile, tile, full, full, full],
        out_shape=[low((rows, D)), f32((rows, FF)), low((rows, FF)), f32((rows, D)), f32((rows, D)), low((rows, D))],
        scratch=[pltpu.VMEM((rows, D), FULL)],
        name="mlp_forward",
    )


def norm_back(values, upstream, gain):
    normal, inverse = normalise(values)
    scaled = upstream * gain
    inner = (
        scaled
        - jnp.mean(scaled, axis=-1, keepdims=True)
        - normal * jnp.mean(scaled * normal, axis=-1, keepdims=True)
    )
    return inverse * inner, upstream * normal


def summed(values):
    return jnp.sum(values, axis=0, keepdims=True)


def mlp_bwd(tick, g, down, mid, branch, c, vec, u, act, wu, wd, g_down, g_up, d_mid, db_out, sums, d_bias_u, dd, total):
    step, last = pl.program_id(0), pl.num_programs(0) - 1
    rows = g.shape[0]
    tick(0)

    @pl.when(step == 0)
    def _():
        sums[...] = jnp.zeros_like(sums)
        for t in tiles(rows):
            grad = g[t, :]
            scaled = grad * row(vec, SCALE_M)
            sums[SCALE_M : SCALE_M + 1, :] += summed(grad * down[t, :])
            sums[BIAS_D : BIAS_D + 1, :] += summed(scaled)
            dd[t, :] = scaled.astype(LOW)
        total[...] = jnp.zeros_like(total)

    g_down[...] = mul_tn(act[...], dd[...]).astype(LOW)
    tick(1)
    d_act = mul_nt(dd[...], wd[...])
    upper = u[...]
    density = jnp.exp(-0.5 * upper * upper) * (2.0 * math.pi) ** (-0.5)
    du = d_act * (phi_of(upper) + upper * density)
    d_bias_u[...] = summed(du)
    du_b = du.astype(LOW)
    tick(2)
    g_up[...] = mul_tn(c[...], du_b).astype(LOW)
    total[...] += mul_nt(du_b, wu[...])

    @pl.when(step == last)
    def _():
        for t in tiles(rows):
            upstream = total[t, :]
            through, gain_terms = norm_back(mid[t, :], upstream, row(vec, GAIN_M))
            sums[GAIN_M : GAIN_M + 1, :] += summed(gain_terms)
            sums[SHIFT_M : SHIFT_M + 1, :] += summed(upstream)
            middle = g[t, :] + through
            d_mid[t, :] = middle
            sums[SCALE_A : SCALE_A + 1, :] += summed(middle * branch[t, :])
            db = middle * row(vec, SCALE_A)
            sums[BIAS_O : BIAS_O + 1, :] += summed(db)
            db_out[t, :] = db.astype(LOW)


def mlp_backward(g, down, mid, branch, c, vec, u, act, w_up, w_down, transfer=None, pace=1, number=0):
    rows = g.shape[0]
    f32, low = lambda s: jax.ShapeDtypeStruct(s, FULL), lambda s: jax.ShapeDtypeStruct(s, LOW)
    full = whole((rows, D))
    tile = columns(rows, FF_TILE)
    return beside(
        mlp_bwd,
        points=3,
        transfer=transfer,
        pace=pace,
        number=number,
        grid=FF // FF_TILE,
        inputs=[g, down, mid, branch, c, vec, u, act, w_up, w_down],
        in_specs=[full] * 5 + [whole(vec.shape), tile, tile, columns(D, FF_TILE), lines(FF_TILE, D)],
        out_specs=[lines(FF_TILE, D), columns(D, FF_TILE), full, full, whole((ROWS, D)), columns(1, FF_TILE)],
        out_shape=[low((FF, D)), low((D, FF)), f32((rows, D)), low((rows, D)), f32((ROWS, D)), f32((1, FF))],
        scratch=[pltpu.VMEM((rows, D), LOW), pltpu.VMEM((rows, D), FULL)],
        name="mlp_backward",
    )


def attend_bwd(tick, d_mid, db, h, a, vec, q, k, v, mixed, wq, wk, wv, wo, gq, gk, gv, go, g_out, sums, d_bias, dq, dk, dv, dm, total):
    step, last = pl.program_id(0), pl.num_programs(0) - 1
    rows = h.shape[0]
    tick(0)

    @pl.when(step == 0)
    def _():
        sums[...] = jnp.zeros_like(sums)
        total[...] = jnp.zeros_like(total)

    dm[...] = mul_nt(db[...], wo[...]).astype(LOW)
    go[...] = mul_tn(mixed[...], db[...]).astype(LOW)
    tick(1)
    lanes, width = lane_sets(), key_set()
    d_bias[...] = jnp.zeros_like(d_bias)

    def image(i, carry):
        at = pl.ds(pl.multiple_of(i * SPAN, SPAN), SPAN)
        for pair in range(GROUP // 128):
            cols = slice(pair * 128, pair * 128 + 128)
            qp, kp, vp, dmp = q[at, cols], k[at, cols], v[at, cols], dm[at, cols]
            grads = []
            for s in range(2):
                prob = softmax_of(qp, kp, lanes[s], width)
                d_prob = mul_nt(jnp.where(lanes[s], dmp, jnp.zeros_like(dmp)), vp)
                ds = (prob * (d_prob - jnp.sum(prob * d_prob, axis=-1, keepdims=True))).astype(LOW)
                grads.append((mul(ds, kp), mul_tn(ds, qp), mul_tn(prob.astype(LOW), dmp)))
            d_q, d_k, d_v = [jnp.where(lanes[0], one, two) for one, two in zip(*grads)]
            d_q, d_k = d_q * HEAD_DIM ** (-0.5), d_k * HEAD_DIM ** (-0.5)
            dq[at, cols], dk[at, cols], dv[at, cols] = d_q.astype(LOW), d_k.astype(LOW), d_v.astype(LOW)
            d_bias[0:1, cols] += summed(d_q)
            d_bias[1:2, cols] += summed(d_v)
        return carry

    images = rows // SPAN
    lax.fori_loop(0, images // 2, image, 0)
    tick(2)
    lax.fori_loop(images // 2, images, image, 0)
    tick(3)
    gq[...] = mul_tn(a[...], dq[...]).astype(LOW)
    gk[...] = mul_tn(a[...], dk[...]).astype(LOW)
    gv[...] = mul_tn(a[...], dv[...]).astype(LOW)
    total[...] += mul_nt(dq[...], wq[...]) + mul_nt(dk[...], wk[...]) + mul_nt(dv[...], wv[...])

    @pl.when(step == last)
    def _():
        for t in tiles(rows):
            upstream = total[t, :]
            through, gain_terms = norm_back(h[t, :], upstream, row(vec, GAIN_A))
            sums[GAIN_A : GAIN_A + 1, :] += summed(gain_terms)
            sums[SHIFT_A : SHIFT_A + 1, :] += summed(upstream)
            g_out[t, :] = d_mid[t, :] + through


def attention_backward(d_mid, db, h, a, vec, q, k, v, mixed, w_in, w_out, transfer=None, pace=1, number=0):
    rows = h.shape[0]
    n = D // GROUP
    f32, low = lambda s: jax.ShapeDtypeStruct(s, FULL), lambda s: jax.ShapeDtypeStruct(s, LOW)
    full = whole((rows, D))
    cols = columns(rows, GROUP)
    weight = columns(D, GROUP)
    return beside(
        attend_bwd,
        points=4,
        transfer=transfer,
        pace=pace,
        number=number,
        grid=n,
        inputs=[d_mid, db, h, a, vec, q, k, v, mixed, w_in, w_in, w_in, w_out],
        in_specs=[full] * 4
        + [whole(vec.shape)]
        + [cols] * 4
        + [columns(D, GROUP, i * n) for i in range(3)]
        + [lines(GROUP, D)],
        out_specs=[weight] * 3 + [lines(GROUP, D), full, whole((ROWS, D)), columns(8, GROUP)],
        out_shape=[low((D, D))] * 4 + [f32((rows, D)), f32((ROWS, D)), f32((8, D))],
        scratch=[pltpu.VMEM((rows, GROUP), LOW)] * 4 + [pltpu.VMEM((rows, D), FULL)],
        name="attention_backward",
    )


GATHER_PIECES = (3, 1, 2, 2)
GATHER_CUTS = (0, 8, 12, 16, 20)
GATHER_PACE = (2, 3, 3, 1)
SCATTER_PIECES = (4, 4)
SCATTER_PACE = (8, 12)


def transfer_alone(transfer, number, name):
    beside(lambda tick: tick(0), 1, transfer, len(transfer.steps), number, 1, [], [], [], [], [], name)


def shape_blocks(shape, term):
    return term.reshape(shape.grid + (term.shape[0] // shape.devices, term.shape[1]))


def spread_rows(tokens):
    return jnp.pad(tokens, ((0, 0), (0, SPAN - SEQ), (0, 0))).reshape(-1, D)


def pack_vectors(mine):
    flat = mine.reshape(-1)
    return jnp.pad(flat, (0, SLAB[0] * SLAB[1] - flat.size)).reshape(SLAB)


def unpack_vectors(slabs, layers, entries):
    flat = slabs.reshape(-1, SLAB[0] * SLAB[1])[:, : layers * entries]
    return flat.reshape(-1, layers, entries).transpose(1, 0, 2).reshape(layers, -1)


def spread_vectors(shape, terms):
    layers, entries = terms.shape
    flat = terms.reshape(layers, shape.devices, -1).transpose(1, 0, 2).reshape(shape.devices, -1)
    flat = jnp.pad(flat, ((0, 0), (0, SLAB[0] * SLAB[1] - flat.shape[1])))
    return flat.reshape(shape.grid + SLAB)


D = 1024
HEADS = 16
HEAD_DIM = 64
FF = 4096
STEP = 10
SEQ = 145


def adamw(weight, gradient, first, second, rate, decay):
    first_new = beta_first * first + (1.0 - beta_first) * gradient
    second_new = beta_second * second + (1.0 - beta_second) * gradient * gradient
    fix_first = 1.0 - beta_first**STEP
    fix_second = 1.0 - beta_second**STEP
    stepped = first_new / fix_first / (jnp.sqrt(second_new / fix_second) + adam_eps)
    return (weight - rate * (stepped + decay * weight), first_new, second_new)


def on_device(
    shape,
    tokens,
    cotangent,
    w_attn_in,
    w_attn_out,
    w_mlp_in,
    w_mlp_out,
    vectors,
    first_attn_in,
    first_attn_out,
    first_mlp_in,
    first_mlp_out,
    first_vectors,
    second_attn_in,
    second_attn_out,
    second_mlp_in,
    second_mlp_out,
    second_vectors,
):
    shards = (w_attn_in, w_attn_out, w_mlp_in, w_mlp_out, vectors)
    layers, images = w_attn_in.shape[0], tokens.shape[0]
    sources = [pack_vectors(vectors.astype(LOW))]
    jobs = []
    for layer in range(layers):
        sources += [shards[m][layer].astype(LOW) for m in range(4)]
        jobs += [[(1 + 4 * layer + m, piece, n)] for m, n in enumerate(GATHER_PIECES) for piece in range(n)]
    jobs[0].append((0, 0, 1))
    held = {}
    cuts = GATHER_CUTS

    def matrix(name):
        return held[name].reshape(-1, held[name].shape[-1])

    def gathering(index):
        return Gathering(shape, sources, jobs, cuts[index], cuts[index + 1], held)

    transfer_alone(gathering(0), 1, "gather")
    rows_of = unpack_vectors(held[0], layers, vectors.shape[1]).astype(FULL).reshape(layers, -1, D)
    hidden = spread_rows(tokens.astype(FULL))
    kept = []
    for layer in range(layers):
        vec, base = rows_of[layer], 1 + 4 * layer
        transfer = gathering(1 + 2 * layer)
        w_in, w_out = matrix(base), matrix(base + 1)
        a, q, k, v, mixed, branch, mid = attention_forward(
            hidden, vec, w_in, w_out, transfer=transfer, pace=GATHER_PACE[2 * layer], number=2 + 2 * layer)
        transfer = gathering(2 + 2 * layer) if layer < layers - 1 else None
        w_up, w_down = matrix(base + 2), matrix(base + 3)
        c, u, act, down, result, low = mlp_forward(
            mid, vec, w_up, w_down, transfer=transfer, pace=GATHER_PACE[2 * layer + 1], number=3 + 2 * layer)
        kept.append((vec, w_in, w_out, w_up, w_down, hidden, a, q, k, v, mixed, branch, mid, c, u, act, down))
        hidden = result
    output = low.reshape(images, SPAN, D)[:, :SEQ]
    grad = spread_rows(cotangent.astype(FULL))
    terms, sums = [None] * layers, [[None] * 6 for _ in range(layers)]
    waiting, number = None, 10
    for layer in reversed(range(layers)):
        vec, w_in, w_out, w_up, w_down, hidden, a, q, k, v, mixed, branch, mid, c, u, act, down = kept[layer]
        transfer = None if waiting is None else Scattering(shape, waiting, (1, 1, 1, 1))
        g_down, g_up, d_mid, db, sums_m, d_bias_u = mlp_backward(
            grad, down, mid, branch, c, vec, u, act, w_up, w_down, transfer=transfer, pace=SCATTER_PACE[0], number=number)
        if transfer is not None:
            sums[layer + 1][:4] = transfer.sums
        transfer = Scattering(shape, [shape_blocks(shape, g) for g in (g_up, g_down)], SCATTER_PIECES)
        g_q, g_k, g_v, g_out, grad, sums_a, d_bias = attention_backward(
            d_mid, db, hidden, a, vec, q, k, v, mixed, w_in, w_out, transfer=transfer, pace=SCATTER_PACE[1], number=number + 1)
        sums[layer][4:] = transfer.sums
        waiting = [shape_blocks(shape, g) for g in (g_q, g_k, g_v, g_out)]
        number += 2
        both = sums_m + sums_a
        terms[layer] = jnp.concatenate(
            [both[:BIAS_Q].reshape(-1), d_bias[:2].reshape(-1), both[BIAS_O:BIAS_U].reshape(-1), d_bias_u.reshape(-1)])
    transfer = Scattering(shape, waiting + [spread_vectors(shape, jnp.stack(terms).astype(LOW))], (1, 1, 1, 1, 1))
    transfer_alone(transfer, number, "scatter")
    sums[0][:4] = transfer.sums[:4]
    stacked = [
        jnp.stack([jnp.concatenate(sums[layer][:3], axis=1) for layer in range(layers)]),
        jnp.stack([sums[layer][3] for layer in range(layers)]),
        jnp.stack([sums[layer][4] for layer in range(layers)]),
        jnp.stack([sums[layer][5] for layer in range(layers)]),
        transfer.sums[4].reshape(-1)[: vectors.size].reshape(vectors.shape),
    ]
    firsts = (first_attn_in, first_attn_out, first_mlp_in, first_mlp_out, first_vectors)
    seconds = (second_attn_in, second_attn_out, second_mlp_in, second_mlp_out, second_vectors)
    settings = (
        (D ** (-0.5), 0.05),
        ((D // 8) ** (-0.5), 0.05),
        (D ** (-0.5), 0.05),
        (FF ** (-0.5), 0.05),
        (0.3, 0.0),
    )
    updated = [
        adamw(
            shards[member],
            stacked[member],
            firsts[member],
            seconds[member],
            settings[member][0],
            settings[member][1],
        )
        for member in range(5)
    ]
    d_tokens = grad.reshape(images, SPAN, D)[:, :SEQ]
    return (
        output,
        d_tokens,
        updated[0][0],
        updated[1][0],
        updated[2][0],
        updated[3][0],
        updated[4][0],
        updated[0][1],
        updated[1][1],
        updated[2][1],
        updated[3][1],
        updated[4][1],
        updated[0][2],
        updated[1][2],
        updated[2][2],
        updated[3][2],
        updated[4][2],
    )


def solution(mesh):
    in_specs = (
        P(("node", "chip"), None, None),
        P(("node", "chip"), None, None),
        P(None, ("node", "chip"), None),
        P(None, ("node", "chip"), None),
        P(None, ("node", "chip"), None),
        P(None, ("node", "chip"), None),
        P(None, ("node", "chip")),
        P(None, ("node", "chip"), None),
        P(None, ("node", "chip"), None),
        P(None, ("node", "chip"), None),
        P(None, ("node", "chip"), None),
        P(None, ("node", "chip")),
        P(None, ("node", "chip"), None),
        P(None, ("node", "chip"), None),
        P(None, ("node", "chip"), None),
        P(None, ("node", "chip"), None),
        P(None, ("node", "chip")),
    )
    out_specs = (
        P(("node", "chip"), None, None),
        P(("node", "chip"), None, None),
        P(None, ("node", "chip"), None),
        P(None, ("node", "chip"), None),
        P(None, ("node", "chip"), None),
        P(None, ("node", "chip"), None),
        P(None, ("node", "chip")),
        P(None, ("node", "chip"), None),
        P(None, ("node", "chip"), None),
        P(None, ("node", "chip"), None),
        P(None, ("node", "chip"), None),
        P(None, ("node", "chip")),
        P(None, ("node", "chip"), None),
        P(None, ("node", "chip"), None),
        P(None, ("node", "chip"), None),
        P(None, ("node", "chip"), None),
        P(None, ("node", "chip")),
    )
    return jax.shard_map(
        functools.partial(on_device, Shape(mesh)), mesh=mesh, in_specs=in_specs, out_specs=out_specs, check_vma=False
    )
```

```python
import functools
import math

import jax
import jax.numpy as jnp
from jax import lax
from jax.experimental import pallas as pl
from jax.experimental.pallas import tpu as pltpu
from jax.sharding import PartitionSpec as P

STEP = 10
beta_first = 0.9
beta_second = 0.999
adam_eps = 1e-08
MESH = pl.DeviceIdType.MESH
ALL = slice(None)
D = 1024
HEADS = 16
HEAD_DIM = 64
FF = 4096
SEQ = 145
SPAN = 160
GROUP = 256
FF_TILE = 512
ROWS = 16
norm_eps = 1e-06
LOW = jnp.bfloat16
FULL = jnp.float32
GAIN_A, SHIFT_A, BIAS_Q, BIAS_V, BIAS_O, SCALE_A, GAIN_M, SHIFT_M, BIAS_D, SCALE_M, BIAS_U = range(11)


class Shape:
    def __init__(self, mesh):
        chips = mesh.shape["chip"]
        self.X = mesh.shape["node"] // 2
        self.Q = 2 ** ((chips.bit_length() - 1) // 2)
        self.P = chips // self.Q
        self.devices = mesh.shape["node"] * chips
        self.grid = (self.X, 2, self.P, self.Q)
        self.sizes = {"x": self.X, "c": 2, "p": self.P, "q": self.Q}


class Place:
    def __init__(self, shape):
        self.sizes = shape.sizes
        node, chip = lax.axis_index("node"), lax.axis_index("chip")
        self.at = {"x": node // 2, "c": lax.rem(node, 2), "p": chip // shape.Q, "q": lax.rem(chip, shape.Q)}
        self.offs, self.devices = {}, {}
        for axis, n in shape.sizes.items():
            for k in range(1, n):
                off = lax.rem(self.at[axis] + k, n)
                to = dict(self.at, **{axis: off})
                self.offs[axis, k] = off
                self.devices[axis, k] = (to["x"] * 2 + to["c"], to["p"] * shape.Q + to["q"])

    def off(self, axis, k):
        return self.offs[axis, k % self.sizes[axis]]

    def greet(self):
        barrier = pltpu.get_barrier_semaphore()
        for device in self.devices.values():
            pl.semaphore_signal(barrier, inc=1, device_id=device, device_id_type=MESH)
        pl.semaphore_wait(barrier, len(self.devices))


class Move:
    def __init__(self, src, dst, came, sems, device):
        if device is None:
            copy = functools.partial(pltpu.make_async_copy, src, dst, sems[0])
            self.start, self.arrived, self.sent = lambda: copy().start(), lambda: copy().wait(), None
        else:
            copy = functools.partial(
                pltpu.make_async_remote_copy,
                send_sem=sems[0], recv_sem=sems[1], device_id=device, device_id_type=MESH)
            self.start = lambda: copy(src, dst).start()
            self.sent = lambda: copy(src, dst).wait_send()
            self.arrived = lambda: copy(came, came).wait_recv()


class Task:
    def __init__(self, place, sems):
        self.place, self.sems, self.used = place, sems, 0
        self.phases = [([], [], []) for _ in range(5)]

    def move(self, begin, end, src, dst, came=None, axis=None, k=None):
        slot, self.used = self.used, self.used + 1
        sems = (self.sems[0].at[slot], self.sems[1].at[slot])
        move = Move(src, dst, dst if came is None else came, sems, None if axis is None else self.place.devices[axis, k])
        self.phases[begin][2].append(move)
        self.phases[end][0].append(move)


def plan(events):
    todo, flying = {}, []
    for time, task, phase in sorted(events, key=lambda e: (e[0], -e[2])):
        waits, work, starts = task.phases[phase]
        acts = todo.setdefault(time, [])
        acts += [move.arrived for move in waits] + work + [move.start for move in starts]
        acts += [move.sent for move in waits if move.sent is not None]
        flying = [move for move in flying if move not in waits] + starts
    return todo, [move.arrived for move in flying] + [move.sent for move in flying if move.sent is not None]


class Gather(Task):
    def __init__(self, place, src, dst, cols, order, sems):
        super().__init__(place, sems)
        at, sizes = place.at, place.sizes
        one, two, three = order

        def region(**fix):
            pick = dict(at, **fix)
            return dst.at[pick["x"], pick["c"], pick["p"], pick["q"], :, cols]

        def push(begin, end, axis, k, own=None, **held):
            came = region(**dict(held, **{axis: place.off(axis, -k)}))
            self.move(begin, end, region(**held) if own is None else own, region(**held), came, axis, k)

        own = src.at[:, cols]
        self.move(0, 1, own, region())
        for k in range(1, sizes[one]):
            push(0, 1, one, k, own)
        for k in range(1, sizes[two]):
            push(1, 2, two, k, **{one: ALL})
        push(1, 4, "c", 1, **{one: ALL})
        for k in range(1, sizes[three]):
            push(2, 3, three, k, **{one: ALL, two: ALL})
        for k in range(1, sizes[two]):
            push(2, 4, "c", 1, **{one: ALL, two: place.off(two, k)})
        for k in range(1, sizes[three]):
            push(3, 4, "c", 1, **{one: ALL, two: ALL, three: place.off(three, k)})


class Scatter(Task):
    def __init__(self, place, src, acc, out, order, bufs, sems, start, stop):
        super().__init__(place, sems)
        at, sizes = place.at, place.sizes
        self.start, self.stop = start, stop
        left = [a for a in "xpq" if a not in order[: max(start - 1, 0)]]

        def held(**fix):
            x, p, q = [fix.get(a, ALL) for a in "xpq"]
            return src.at[x, at["c"], p, q] if acc is None else acc.at[tuple(fix.get(a, ALL) for a in left)]

        def add(view, terms):
            if len(terms) == 1:
                view[...] = view[...] + terms[0][...]
            else:
                view[...] = sum([term[...].astype(FULL) for term in terms], view[...].astype(FULL)).astype(LOW)

        def finish():
            last = order[2]
            total = held(**at)[...].astype(FULL)
            for k in range(1, sizes[last]):
                total = total + bufs[3][k - 1].astype(FULL)
            out[...] = total

        if start > 0:
            self.move(start - 1, start, src, acc)
        else:
            if acc is not None:
                self.move(0, 1, src.at[:, at["c"]], acc)
            self.move(0, 1, src.at[:, place.off("c", 1)], bufs[0], None, "c", 1)
            for i in range(sizes["x"]):
                self.phases[1][1].append(functools.partial(add, held(x=i), [bufs[0].at[i]]))
        known = {}
        for phase, axis in enumerate(order, 1):
            if phase >= start:
                for k in range(1, sizes[axis]):
                    away = held(**dict(known, **{axis: place.off(axis, k)}))
                    if phase < stop:
                        self.move(phase, phase + 1, away, bufs[phase].at[k - 1], None, axis, k)
            known[axis] = at[axis]
            if start <= phase < min(3, stop):
                terms = [bufs[phase].at[k - 1] for k in range(1, sizes[axis])]
                self.phases[phase + 1][1].append(functools.partial(add, held(**known), terms))
        if stop > 4:
            self.phases[4][1].append(finish)
        self.left_over = held(**{a: at[a] for a in order[: max(stop - 1, 0)]})


class Spill(Task):
    def __init__(self, place, src, dst, sems):
        super().__init__(place, sems)
        self.move(0, 1, src, dst)


class Total(Task):
    def __init__(self, place, src, out, bufs, sems):
        super().__init__(place, sems)
        stages = [src] + list(bufs[4:]) + [out]

        def add(i):
            total = stages[i][...]
            for k in range(1, place.sizes["cxqp"[i]]):
                total = total + bufs[i][k - 1]
            stages[i + 1][...] = total

        for i, axis in enumerate("cxqp"):
            for k in range(1, place.sizes[axis]):
                self.move(i, i + 1, stages[i], bufs[i].at[k - 1], None, axis, k)
            self.phases[i + 1][1].append(functools.partial(add, i))


ANYWHERE = pl.BlockSpec(memory_space=pl.ANY)


ORDERS = (("x", "q", "p"), ("q", "x", "p")) * 2 + (("x", "p", "q"), ("q", "p", "x"))


class Piece:
    def __init__(self, block, source, order):
        self.block, self.source, self.order, self.done, self.sum = block, source, ORDERS[order % len(ORDERS)], 0, None


class Scattering:
    def __init__(self, shape, ticks, entries, spills=(), total=None, last=False):
        self.shape, self.ticks, self.spills, self.total = shape, ticks, spills, total
        self.aliases, self.scratch, self.inputs, self.made = {}, [], [], []
        self.out_shape, self.out_specs = [], []
        sizes = shape.sizes
        blocks = {}
        for piece, tick, lag in entries:
            first = piece.done
            times = {f: tick + lag * f for f in range(5)} if first == 0 else {
                f: tick if f < first else tick + 1 + lag * (f - first) for f in range(first - 1, 5)}
            stop = 5 if last else min([f for f, time in times.items() if time >= ticks] + [5])
            stop = 5 if stop == 4 else stop
            buffers, index = {}, {}
            if piece.source[0] != "own":
                axes = [sizes[a] for a in "xpq" if a not in piece.order[: max(first - 1, 0)]]
                buffers["acc"] = tuple(axes) + piece.block
            if first == 0:
                buffers[0] = tuple(sizes[a] for a in "xpq") + piece.block
            for f, axis in enumerate(piece.order, 1):
                if first <= f < stop:
                    rest = [sizes[a] for a in "xpq" if a not in piece.order[:f]]
                    buffers[f] = (sizes[axis] - 1, *rest) + piece.block
            for key, buffer in buffers.items():
                index[key] = len(self.scratch)
                self.scratch.append(pltpu.VMEM(buffer, LOW))
            if piece.source[0] != "own" and not any(piece.source[1] is a for a in self.inputs):
                self.inputs.append(piece.source[1])
            if stop == 5:
                blocks.setdefault(piece.block, []).append(piece)
            self.made.append([piece, times, stop, index])
        for block, pieces in blocks.items():
            for i, piece in enumerate(pieces):
                piece.target = (len(self.out_shape), i)
            self.out_shape.append(jax.ShapeDtypeStruct((len(pieces),) + block, FULL))
            self.out_specs.append(whole(self.out_shape[-1].shape))
        for piece, _, stop, _ in self.made:
            if stop < 5:
                piece.target = (len(self.out_shape), None)
                axes = [sizes[a] for a in "xpq" if a not in piece.order[: stop - 1]]
                self.out_shape.append(jax.ShapeDtypeStruct(tuple(axes) + piece.block, LOW))
                self.out_specs.append(ANYWHERE)
        self.first_spill = len(self.out_shape)
        for _, _, _, block in spills:
            self.out_shape.append(jax.ShapeDtypeStruct(block, LOW))
            self.out_specs.append(ANYWHERE)
        if total is not None:
            self.first_total = len(self.scratch)
            self.scratch += [pltpu.VMEM((sizes[a] - 1,) + total[1], FULL) for a in "cxqp"]
            self.scratch += [pltpu.VMEM(total[1], FULL)] * 3
            self.out_shape.append(jax.ShapeDtypeStruct(total[1], FULL))
            self.out_specs.append(whole(total[1]))
        self.in_specs = [ANYWHERE] * len(self.inputs)
        copies = max(3 + sum(sizes[a] - 1 for a in "xpq"), sum(n - 1 for n in sizes.values()))
        self.scratch += [pltpu.SemaphoreType.DMA((len(self.made) + len(spills) + 1, copies))] * 2

    def build(self, ins, outs, scratch, own):
        place = Place(self.shape)
        send, recv = scratch[-2:]
        events, halted, slot = [], [], 0
        for piece, times, stop, index in self.made:
            kind, base, lead = piece.source
            if kind == "own":
                src = own[base].at[lead]
            else:
                src = ins[[a is base for a in self.inputs].index(True)]
                src = src if lead is None else src.at[lead]
            bufs = {key: scratch[i] for key, i in index.items()}
            o, i = piece.target
            out = outs[o].at[i] if stop == 5 else outs[o]
            task = Scatter(
                place, src, bufs.get("acc"), out, piece.order, bufs, (send.at[slot], recv.at[slot]), piece.done, stop)
            slot += 1
            events += [(time, task, f) for f, time in times.items() if f < stop]
            if stop < 5:
                halted.append((task, out))
        for n, (tick, base, lead, _) in enumerate(self.spills):
            task = Spill(place, own[base].at[lead], outs[self.first_spill + n], (send.at[slot], recv.at[slot]))
            slot += 1
            events.append((tick, task, 0))
        if self.total is not None:
            task = Total(
                place, own[self.total[0]], outs[-1], scratch[self.first_total : -2], (send.at[slot], recv.at[slot]))
            events += [(self.ticks + 2 * f, task, f) for f in range(5)]
        todo, rest = plan(events)
        moves = []
        for task, out in halted:
            rest += task.phases[task.stop][1]
            move = Move(task.left_over, out, None, (task.sems[0].at[task.used],), None)
            rest.append(move.start)
            moves.append(move.arrived)
        return place, todo, rest + moves

    def take(self, outs):
        for piece, _, stop, _ in self.made:
            o, i = piece.target
            if stop == 5:
                piece.sum = (outs[o], i)
            else:
                piece.source, piece.done = ("part", outs[o], None), stop
        self.spilled = outs[self.first_spill : self.first_spill + len(self.spills)]
        self.result = outs[-1]


def beside(kernel, points, transfer, number, grid, inputs, in_specs, out_specs, out_shape, scratch, name, limit=62):
    total = grid * points
    counts = [len(inputs), len(transfer.inputs) if transfer else 0, len(out_shape), len(transfer.out_shape) if transfer else 0, len(scratch)]

    def body(*refs):
        groups, i = [], 0
        for n in counts:
            groups.append(refs[i : i + n])
            i += n
        groups.append(refs[i:])
        step = pl.program_id(0)
        if transfer is None:
            kernel(lambda point: None, *groups[0], *groups[2], *groups[4])
            return
        place, todo, rest = transfer.build(groups[1], groups[3], groups[5], groups[4])

        def tick(point):
            if point == 0:
                pl.when(step == 0)(place.greet)
            for time in sorted(todo):
                if time < total and time % points == point:
                    @pl.when(step == time // points)
                    def _():
                        for act in todo[time]:
                            act()

        kernel(tick, *groups[0], *groups[2], *groups[4])

        @pl.when(step == grid - 1)
        def _():
            for act in [act for time in sorted(todo) if time >= total for act in todo[time]] + rest:
                act()

    extra = {}
    if transfer is not None:
        extra["input_output_aliases"] = {counts[0] + i: counts[2] + o for i, o in transfer.aliases.items()}
        inputs, in_specs = list(inputs) + transfer.inputs, list(in_specs) + transfer.in_specs
        out_specs, out_shape = list(out_specs) + transfer.out_specs, list(out_shape) + transfer.out_shape
        scratch = list(scratch) + transfer.scratch
    outs = pl.pallas_call(
        body,
        grid=(grid,),
        in_specs=in_specs,
        out_specs=out_specs,
        out_shape=out_shape,
        scratch_shapes=scratch,
        name=name,
        compiler_params=pltpu.CompilerParams(
            dimension_semantics=("arbitrary",),
            vmem_limit_bytes=limit * 2**20,
            collective_id=None if transfer is None else number,
            has_side_effects=transfer is not None,
        ),
        **extra,
    )(*inputs)
    if transfer is not None:
        transfer.take(outs[counts[2] :])
    return outs[: counts[2]]


def mul(a, b):
    return jnp.dot(a, b, preferred_element_type=FULL)


def mul_nt(a, b):
    return lax.dot_general(a, b, (((1,), (1,)), ((), ())), preferred_element_type=FULL)


def mul_tn(a, b):
    return lax.dot_general(a, b, (((0,), (0,)), ((), ())), preferred_element_type=FULL)


def normalise(values):
    centred = values - jnp.mean(values, axis=-1, keepdims=True)
    inverse = lax.rsqrt(jnp.mean(centred * centred, axis=-1, keepdims=True) + norm_eps)
    return centred * inverse, inverse


def tiles(rows, step=160):
    return [slice(i, i + step) for i in range(0, rows, step)]


def row(vec, index):
    return vec[index : index + 1, :]


def softmax_of(q, k, lanes, width):
    scores = mul_nt(jnp.where(lanes, q, jnp.zeros_like(q)), k) * HEAD_DIM ** (-0.5)
    scores = jnp.where(width, scores, -1e30)
    expo = jnp.exp(scores - jnp.max(scores, axis=-1, keepdims=True))
    return expo * (1.0 / jnp.sum(expo, axis=-1, keepdims=True))


def lane_sets():
    lane = lax.broadcasted_iota(jnp.int32, (SPAN, 128), 1)
    return [lane < HEAD_DIM, lane >= HEAD_DIM]


def key_set():
    return lax.broadcasted_iota(jnp.int32, (SPAN, SPAN), 1) < SEQ


def whole(shape):
    return pl.BlockSpec(shape, lambda j: (0,) * len(shape), pipeline_mode=pl.Buffered(1))


def whole_of(layer, rows):
    return pl.BlockSpec((None, rows, D), lambda j: (layer, 0, 0), pipeline_mode=pl.Buffered(1))


def columns_of(layer, rows, width):
    return pl.BlockSpec((None, rows, width), lambda j: (layer, 0, j))


def columns(rows, width, at=0):
    return pl.BlockSpec((rows, width), lambda j: (0, j + at))


def lines(height, cols):
    return pl.BlockSpec((height, cols), lambda j: (j, 0))


def phi_of(u):
    return 0.5 * (1.0 + lax.erf(u * 0.5**0.5))


N_IN, N_UP, N_DOWN = D // GROUP, FF // FF_TILE, D // GROUP
ITEMS = N_IN + 1 + N_UP + N_DOWN
GATHER_LAG = 3
AHEAD = 4 * GATHER_LAG + 1
GATHER_ORDERS = (("p", "q", "x"), ("p", "x", "q")) * 2 + (("q", "p", "x"), ("x", "p", "q"))


def item_of(number):
    if number < N_IN:
        return 0, number, pl.ds(number * 3 * GROUP, 3 * GROUP)
    number -= N_IN
    if number == 0:
        return 1, 0, pl.ds(0, D)
    number -= 1
    if number < N_UP:
        return 2, number, pl.ds(number * FF_TILE, FF_TILE)
    return 3, number - N_UP, pl.ds((number - N_UP) * GROUP, GROUP)


def matrix_of(ref):
    value = ref[...]
    flat = (-1, value.shape[-1])
    return value.reshape(flat) if value.shape[-2] % 16 == 0 else value.astype(FULL).reshape(flat).astype(LOW)


def forward_kernel(shape, layers, *refs):
    count = 4 * layers
    tokens, packed, *sources = refs[: 2 + count]
    refs = refs[2 + count :]
    a_out, q_out, k_out, v_out, mixed_out, branch_out, mid_out, c_out, u_out, act_out, down_out, vec_out, next_out, low_out = refs[:14]
    gathered, refs = refs[14 : 14 + count], refs[14 + count :]
    h, act, vec = refs[:3]
    slots, sums, (send, recv, loaded) = refs[3:7], refs[7:14], refs[14:]
    step = pl.program_id(0)
    rows = h.shape[0]
    place = Place(shape)
    total = layers * ITEMS
    jobs, loads, n = [], [], 1
    for layer in range(layers):
        for number in range(ITEMS):
            weight, index, cols = item_of(number)
            src, dst = sources[4 * layer + weight], gathered[4 * layer + weight]
            half, job = cols.size // 2, []
            for i in range(2):
                part = pl.ds(cols.start + i * half, half)
                order = GATHER_ORDERS[(n - 1) % len(GATHER_ORDERS)]
                job.append(Gather(place, src, dst, part, order, (send.at[n], recv.at[n])))
                n += 1
            jobs.append(job)
            slot = index % slots[weight].shape[0]
            loads.append(
                functools.partial(
                    pltpu.make_async_copy, dst.at[:, :, :, :, :, cols], slots[weight].at[slot], loaded.at[weight, slot]))
    jobs[0].append(Total(place, packed, vec_out, sums, (send.at[0], recv.at[0])))
    todo, _ = plan([
        (i + GATHER_LAG * phase, task, phase) for i, job in enumerate(jobs) for task in job for phase in range(5)])

    pl.when(step == 0)(place.greet)
    for s in range(total + AHEAD):
        @pl.when(step == s)
        def _():
            if 0 <= s - AHEAD < total:
                loads[s - AHEAD]().wait()
            for act in todo.get(s, []):
                act()
            if 0 <= s - AHEAD + 1 < total:
                loads[s - AHEAD + 1]().start()

    at = step - AHEAD
    item = jnp.maximum(lax.rem(jnp.maximum(at, 0), ITEMS), 0)
    layer = jnp.maximum(at, 0) // ITEMS
    live = at >= 0
    base = pl.multiple_of(layer * ROWS, ROWS)

    def line(index):
        return vec[pl.ds(index, 1), :]

    @pl.when(at == 0)
    def _():
        h[...] = tokens[...]

    @pl.when(live & (item == 0))
    def _():
        vec[...] = vec_out[pl.ds(base, ROWS), :]
        for t in tiles(rows):
            normal, _ = normalise(h[t, :])
            a_out[0, t, :] = (normal * line(GAIN_A) + line(SHIFT_A)).astype(LOW)

    @pl.when(live & (item < N_IN))
    def _():
        group = pl.ds(pl.multiple_of(item * GROUP, GROUP), GROUP)
        proj = mul(a_out[0], matrix_of(slots[0].at[lax.rem(item, 2)]))
        q_out[0] = (proj[:, :GROUP] + vec[BIAS_Q : BIAS_Q + 1, group]).astype(LOW)
        k_out[0] = proj[:, GROUP : 2 * GROUP].astype(LOW)
        v_out[0] = (proj[:, 2 * GROUP :] + vec[BIAS_V : BIAS_V + 1, group]).astype(LOW)
        lanes, width = lane_sets(), key_set()

        def image(i, carry):
            t = pl.ds(pl.multiple_of(i * SPAN, SPAN), SPAN)
            done = []
            for pair in range(GROUP // 128):
                cols = slice(pair * 128, pair * 128 + 128)
                q, k, v = q_out[0, t, cols], k_out[0, t, cols], v_out[0, t, cols]
                both = [mul(softmax_of(q, k, lanes[s], width).astype(LOW), v) for s in range(2)]
                done.append(jnp.where(lanes[0], both[0], both[1]).astype(LOW))
            mixed_out[0, t, group] = jnp.concatenate(done, axis=1)
            return carry

        lax.fori_loop(0, rows // SPAN, image, 0)

    @pl.when(live & (item == N_IN))
    def _():
        weight = matrix_of(slots[1].at[0])
        for t in tiles(rows):
            branch = mul(mixed_out[0, t, :], weight) + line(BIAS_O)
            branch_out[0, t, :] = branch
            middle = h[t, :] + line(SCALE_A) * branch
            mid_out[0, t, :] = middle
            normal, _ = normalise(middle)
            c_out[0, t, :] = (normal * line(GAIN_M) + line(SHIFT_M)).astype(LOW)

    @pl.when(live & (item > N_IN) & (item <= N_IN + N_UP))
    def _():
        tile = item - N_IN - 1
        per = D // FF_TILE
        bias = vec[pl.ds(BIAS_U + tile // per, 1), pl.ds(pl.multiple_of(lax.rem(tile, per) * FF_TILE, FF_TILE), FF_TILE)]
        u = mul(c_out[0], matrix_of(slots[2].at[lax.rem(tile, 2)])) + bias
        u_out[0] = u
        active = (u * phi_of(u)).astype(LOW)
        act_out[0] = active
        act[:, pl.ds(pl.multiple_of(tile * FF_TILE, FF_TILE), FF_TILE)] = active

    @pl.when(live & (item > N_IN + N_UP))
    def _():
        tile = item - N_IN - 1 - N_UP
        group = pl.ds(pl.multiple_of(tile * GROUP, GROUP), GROUP)
        down = mul(act[...], matrix_of(slots[3].at[lax.rem(tile, 2)])) + vec[BIAS_D : BIAS_D + 1, group]
        down_out[0, :, group] = down
        h[:, group] = mid_out[0, :, group] + vec[SCALE_M : SCALE_M + 1, group] * down

    @pl.when(at == ITEMS - 1)
    def _():
        next_out[...] = h[...]

    @pl.when(at == total - 1)
    def _():
        low_out[...] = h[...].astype(LOW)


def forward(shape, layers, tokens, packed, sources, number):
    rows = tokens.shape[0]
    total = layers * ITEMS

    def spot(s):
        at = jnp.clip(s - AHEAD, 0, total - 1)
        return at // ITEMS, lax.rem(at, ITEMS)

    def out(width, dtype, pick=None, block=D):
        def index(s):
            layer, item = spot(s)
            return layer, 0, 0 if pick is None else pick(item)

        return jax.ShapeDtypeStruct((layers, rows, width), dtype), pl.BlockSpec((1, rows, block), index)

    def one(spec_shape, dtype):
        return jax.ShapeDtypeStruct(spec_shape, dtype), whole(spec_shape)

    group = lambda item: jnp.minimum(item, N_IN - 1)
    tile = lambda item: jnp.clip(item - N_IN - 1, 0, N_UP - 1)
    qkv = [out(D, LOW, group, GROUP)] * 3
    outs = [out(D, LOW)] + qkv + [out(D, LOW), out(D, FULL), out(D, FULL), out(D, LOW)]
    outs += [out(FF, FULL, tile, FF_TILE), out(FF, LOW, tile, FF_TILE), out(D, FULL)]
    outs += [one(packed.shape, FULL), one((rows, D), FULL), one((rows, D), LOW)]
    outs += [(jax.ShapeDtypeStruct(shape.grid + b.shape, LOW), ANYWHERE) for b in sources]
    sizes = shape.sizes
    tasks = 2 * total + 1
    copies = 1 + sum(sizes[a] - 1 for a in "xpq") + 1 + 2 * (max(sizes.values()) - 1)
    deep = [b.shape[0] for b in sources[:4]]
    slots = [
        pltpu.VMEM((count,) + shape.grid + (depth, width), LOW)
        for count, depth, width in zip((2, 1, 2, 2), deep, (3 * GROUP, D, FF_TILE, GROUP))
    ]
    return pl.pallas_call(
        functools.partial(forward_kernel, shape, layers),
        grid=(total + AHEAD,),
        in_specs=[whole((rows, D)), whole(packed.shape)] + [ANYWHERE] * len(sources),
        out_specs=[o[1] for o in outs],
        out_shape=[o[0] for o in outs],
        scratch_shapes=[pltpu.VMEM((rows, D), FULL), pltpu.VMEM((rows, FF), LOW), pltpu.VMEM((ROWS, D), FULL)]
        + slots
        + [pltpu.VMEM((sizes[a] - 1,) + packed.shape, FULL) for a in "cxqp"]
        + [pltpu.VMEM(packed.shape, FULL)] * 3
        + [pltpu.SemaphoreType.DMA((tasks, copies))] * 2
        + [pltpu.SemaphoreType.DMA((4, 2))],
        name="forward",
        compiler_params=pltpu.CompilerParams(
            dimension_semantics=("arbitrary",), vmem_limit_bytes=60 * 2**20, collective_id=number, has_side_effects=True),
    )(tokens, packed, *sources)


def norm_back(values, upstream, gain):
    normal, inverse = normalise(values)
    scaled = upstream * gain
    inner = (
        scaled
        - jnp.mean(scaled, axis=-1, keepdims=True)
        - normal * jnp.mean(scaled * normal, axis=-1, keepdims=True)
    )
    return inverse * inner, upstream * normal


def summed(values):
    return jnp.sum(values, axis=0, keepdims=True)


def mlp_bwd(tick, g, down, mid, branch, c, vec, u, act, wu, wd, g_down, d_mid, db_out, sums, d_bias_u, dd, stage):
    step, last = pl.program_id(0), pl.num_programs(0) - 1
    rows = g.shape[0]
    tick(0)

    @pl.when(step == 0)
    def _():
        sums[...] = jnp.zeros_like(sums)
        for t in tiles(rows):
            grad = g[t, :]
            scaled = grad * row(vec, SCALE_M)
            sums[SCALE_M : SCALE_M + 1, :] += summed(grad * down[t, :])
            sums[BIAS_D : BIAS_D + 1, :] += summed(scaled)
            dd[t, :] = scaled.astype(LOW)
        d_mid[...] = jnp.zeros_like(d_mid)

    d_act = mul_nt(dd[...], wd[...])
    upper = u[...]
    density = jnp.exp(-0.5 * upper * upper) * (2.0 * math.pi) ** (-0.5)
    du = d_act * (phi_of(upper) + upper * density)
    d_bias_u[...] = summed(du)
    du_b = du.astype(LOW)
    stage[step] = mul_tn(c[...], du_b).reshape(stage.shape[1:]).astype(LOW)
    tick(1)
    g_down[...] = mul_tn(act[...], dd[...]).astype(LOW)
    d_mid[...] += mul_nt(du_b, wu[...])

    @pl.when(step == last)
    def _():
        for t in tiles(rows):
            upstream = d_mid[t, :]
            through, gain_terms = norm_back(mid[t, :], upstream, row(vec, GAIN_M))
            sums[GAIN_M : GAIN_M + 1, :] += summed(gain_terms)
            sums[SHIFT_M : SHIFT_M + 1, :] += summed(upstream)
            middle = g[t, :] + through
            d_mid[t, :] = middle
            sums[SCALE_A : SCALE_A + 1, :] += summed(middle * branch[t, :])
            db = middle * row(vec, SCALE_A)
            sums[BIAS_O : BIAS_O + 1, :] += summed(db)
            db_out[t, :] = db.astype(LOW)


def mlp_backward(layer, g, down, mid, branch, c, vec, u, act, w_up, w_down, shape, transfer, number):
    rows = g.shape[0]
    f32, low = lambda s: jax.ShapeDtypeStruct(s, FULL), lambda s: jax.ShapeDtypeStruct(s, LOW)
    full = whole((rows, D))
    tile = columns_of(layer, rows, FF_TILE)
    steps = FF // FF_TILE
    return beside(
        mlp_bwd,
        points=MLP_POINTS,
        transfer=transfer,
        number=number,
        grid=steps,
        inputs=[g, down, mid, branch, c, vec, u, act, w_up, w_down],
        in_specs=[full] + [whole_of(layer, rows)] * 4
        + [whole(vec.shape), tile, tile, columns(D, FF_TILE), lines(FF_TILE, D)],
        out_specs=[lines(FF_TILE, D), full, full, whole((ROWS, D)), columns(1, FF_TILE)],
        out_shape=[low((FF, D)), f32((rows, D)), low((rows, D)), f32((ROWS, D)), f32((1, FF))],
        scratch=[
            pltpu.VMEM((rows, D), LOW),
            pltpu.VMEM((steps,) + shape.grid + (D // shape.devices, FF_TILE), LOW),
        ],
        name="mlp_backward",
    )


def attend_bwd(tick, d_mid, db, h, a, vec, mixed, rest, q, k, v, wq, wk, wv, wo, g_out, sums, dq, dk, dv, dm, stage, values):
    step, last = pl.program_id(0), pl.num_programs(0) - 1
    rows = h.shape[0]
    tick(0)

    @pl.when(step == 0)
    def _():
        sums[...] = jnp.zeros_like(sums)
        g_out[...] = jnp.zeros_like(g_out)

    def store(kind, term):
        stage[step, kind] = term.reshape(stage.shape[2:]).astype(LOW)

    group = pl.ds(pl.multiple_of(step * GROUP, GROUP), GROUP)
    dm[...] = mul_nt(db[...], wo[...]).astype(LOW)
    store(3, mul_tn(mixed[...], db[:, group]))
    lanes, width = lane_sets(), key_set()

    def image(i, carry):
        at = pl.ds(pl.multiple_of(i * SPAN, SPAN), SPAN)
        bias = []
        for pair in range(GROUP // 128):
            cols = slice(pair * 128, pair * 128 + 128)
            qp, kp, vp, dmp = q[at, cols], k[at, cols], v[at, cols], dm[at, cols]
            grads = []
            for s in range(2):
                prob = softmax_of(qp, kp, lanes[s], width)
                d_prob = mul_nt(jnp.where(lanes[s], dmp, jnp.zeros_like(dmp)), vp)
                ds = (prob * (d_prob - jnp.sum(prob * d_prob, axis=-1, keepdims=True))).astype(LOW)
                grads.append((mul(ds, kp), mul_tn(ds, qp), mul_tn(prob.astype(LOW), dmp)))
            d_q, d_k, d_v = [jnp.where(lanes[0], one, two) for one, two in zip(*grads)]
            d_q, d_k = d_q * HEAD_DIM ** (-0.5), d_k * HEAD_DIM ** (-0.5)
            dq[at, cols], dk[at, cols], dv[at, cols] = d_q.astype(LOW), d_k.astype(LOW), d_v.astype(LOW)
            bias.append((summed(d_q), summed(d_v)))
        sums[BIAS_Q : BIAS_Q + 1, group] += jnp.concatenate([b[0] for b in bias], axis=1)
        sums[BIAS_V : BIAS_V + 1, group] += jnp.concatenate([b[1] for b in bias], axis=1)
        return carry

    images = rows // SPAN
    lax.fori_loop(0, images // 2, image, 0)
    tick(1)
    lax.fori_loop(images // 2, images, image, 0)
    for kind, term in enumerate((dq, dk, dv)):
        store(kind, mul_tn(a[...], term[...]))
    tick(2)
    g_out[...] += mul_nt(dq[...], wq[...]) + mul_nt(dk[...], wk[...]) + mul_nt(dv[...], wv[...])

    @pl.when(step == last)
    def _():
        for t in tiles(rows):
            upstream = g_out[t, :]
            through, gain_terms = norm_back(h[t, :], upstream, row(vec, GAIN_A))
            sums[GAIN_A : GAIN_A + 1, :] += summed(gain_terms)
            sums[SHIFT_A : SHIFT_A + 1, :] += summed(upstream)
            g_out[t, :] = d_mid[t, :] + through
        values[...] = rest[...]
        values[:ROWS, :] += sums[...]


def attention_backward(layer, d_mid, db, h, a, vec, mixed, rest, q, k, v, w_in, w_out, shape, transfer, number):
    rows = h.shape[0]
    n = D // GROUP
    f32 = lambda s: jax.ShapeDtypeStruct(s, FULL)
    full = whole((rows, D))
    cols = columns_of(layer, rows, GROUP)
    return beside(
        attend_bwd,
        points=ATTEND_POINTS,
        transfer=transfer,
        number=number,
        grid=n,
        inputs=[d_mid, db, h, a, vec, mixed, rest, q, k, v, w_in, w_in, w_in, w_out],
        in_specs=[full] * 3
        + [whole_of(layer, rows), whole(vec.shape), whole_of(layer, rows), whole(rest.shape)]
        + [cols] * 3
        + [pl.BlockSpec((D, GROUP), lambda j, m=m: (0, 3 * j + m)) for m in range(3)]
        + [lines(GROUP, D)],
        out_specs=[full, whole((ROWS, D))],
        out_shape=[f32((rows, D)), f32((ROWS, D))],
        scratch=[pltpu.VMEM((rows, GROUP), LOW)] * 4
        + [
            pltpu.VMEM((n, 4) + shape.grid + (D // shape.devices, GROUP), LOW),
            pltpu.VMEM(rest.shape, FULL),
        ],
        name="attention_backward",
    )


MLP_POINTS, MLP_LAG = 2, 3
ATTEND_POINTS = 3
TOP_LAG = 2
END_LAG = 2
MLP_TICKS, ATTEND_TICKS = MLP_POINTS * N_UP, ATTEND_POINTS * N_IN
TOP_UP = (1, 3, 5, 7, 9, 11, 13, 15)
TOP_DOWN = (1, 2, 5, 6, 9, 10, 11, 11)
TOP_IN = (3, 4, 7, 8)
LOW_LEFT = (2, 3, 5, 6)
LOW_UP = (7, 9, 11, 13, 14, 15)
END_LEFT = (1, 2)
END_DOWN = (2, 3, 5, 6, 8, 9, 10, 10)
END_IN = (4, 4, 7, 7, 9, 9, 11, 11)


def resumed(pieces, lag):
    under_way = [piece for piece in pieces if piece.sum is None]
    return [(piece, i // 8, lag) for i, piece in enumerate(under_way)]


def shape_blocks(shape, term):
    return term.reshape(shape.grid + (term.shape[0] // shape.devices, term.shape[1]))


def spread_rows(tokens):
    return jnp.pad(tokens, ((0, 0), (0, SPAN - SEQ), (0, 0))).reshape(-1, D)


def adamw(weight, gradient, first, second, rate, decay):
    first_new = beta_first * first + (1.0 - beta_first) * gradient
    second_new = beta_second * second + (1.0 - beta_second) * gradient * gradient
    fix_first = 1.0 - beta_first**STEP
    fix_second = 1.0 - beta_second**STEP
    stepped = first_new / fix_first / (jnp.sqrt(second_new / fix_second) + adam_eps)
    return (weight - rate * (stepped + decay * weight), first_new, second_new)


def on_device(
    shape,
    tokens,
    cotangent,
    w_attn_in,
    w_attn_out,
    w_mlp_in,
    w_mlp_out,
    vectors,
    first_attn_in,
    first_attn_out,
    first_mlp_in,
    first_mlp_out,
    first_vectors,
    second_attn_in,
    second_attn_out,
    second_mlp_in,
    second_mlp_out,
    second_vectors,
):
    shards = (w_attn_in, w_attn_out, w_mlp_in, w_mlp_out, vectors)
    layers, images = w_attn_in.shape[0], tokens.shape[0]
    mine = lax.axis_index(("node", "chip")) * vectors.shape[1]
    entries = D * (BIAS_U + FF // D)
    packed = lax.dynamic_update_slice_in_dim(
        jnp.zeros((layers, entries), FULL), lax.reduce_precision(vectors, 8, 7), mine, axis=1)
    packed = jnp.pad(packed, ((0, 0), (0, D * ROWS - entries))).reshape(layers * ROWS, D)
    sources = []
    for layer in range(layers):
        by_group = shards[0][layer].reshape(-1, 3, D // GROUP, GROUP).transpose(0, 2, 1, 3).reshape(-1, 3 * D)
        sources += [m.astype(LOW) for m in (by_group, w_attn_out[layer], w_mlp_in[layer], w_mlp_out[layer])]
    first = spread_rows(tokens.astype(FULL))
    outs = forward(shape, layers, first, packed, sources, 1)
    vec_rows, second, low = outs[11:14]
    weights = [w.reshape(-1, w.shape[-1]) for w in outs[14:]]
    kept = []
    for layer in range(layers):
        a, q, k, v, mixed, branch, mid, c, u, act, down = outs[:11]
        vec = vec_rows[layer * ROWS : layer * ROWS + ROWS]
        hidden = second if layer else first
        kept.append((vec, *weights[4 * layer : 4 * layer + 4], hidden, a, q, k, v, mixed, branch, mid, c, u, act, down))
    output = low.reshape(images, SPAN, D)[:, :SEQ]
    grad = spread_rows(cotangent.astype(FULL))
    high, deep = D // shape.devices, FF // shape.devices
    pieces, rest, left, number, order = [], jnp.zeros((0, D), FULL), [], 10, 0
    everything = [[[None] * (2 * N_UP), [None] * N_DOWN * 2, [None] * 4 * N_IN] for _ in range(layers)]

    def piece(layer, matrix, index, block, source):
        made = everything[layer][matrix][index] = Piece(block, source, index)
        pieces.append(made)
        return made

    for layer in reversed(range(layers)):
        vec, w_in, w_out, w_up, w_down, hidden, a, q, k, v, mixed, branch, mid, c, u, act, down = kept[layer]
        top = layer == layers - 1
        entries = resumed(pieces, MLP_LAG)
        for i, one in enumerate(left):
            entries.append((one, LOW_LEFT[i // 2], MLP_LAG))
        starts = TOP_UP if top else LOW_UP
        half = FF_TILE // 2
        for tile, start in enumerate(starts):
            for i in range(2):
                source = ("own", 1, (tile, ALL, ALL, ALL, ALL, ALL, pl.ds(i * half, half)))
                entries.append((piece(layer, 0, 2 * tile + i, (high, half), source), start, MLP_LAG))
        spills = [
            (MLP_TICKS, 1, tile, shape.grid + (high, FF_TILE)) for tile in range(len(starts), N_UP)]
        transfer = Scattering(shape, MLP_TICKS, entries, spills)
        g_down, d_mid, db, sums_m, d_bias_u = mlp_backward(
            layer, grad, down, mid, branch, c, vec, u, act, w_up, w_down, shape, transfer, number)
        lag = TOP_LAG if layer else END_LAG
        entries = resumed(pieces, lag)
        for n, tile in enumerate(range(len(starts), N_UP)):
            for i in range(2):
                source = ("hbm", transfer.spilled[n], (ALL, ALL, ALL, ALL, ALL, pl.ds(i * half, half)))
                entries.append((piece(layer, 0, 2 * tile + i, (high, half), source), END_LEFT[n], lag))
        spare = jnp.zeros((ROWS - BIAS_U - FF // D, D), FULL)
        rest = jnp.concatenate([sums_m[:BIAS_U], d_bias_u.reshape(-1, D), spare, rest])
        rest = jnp.pad(rest, ((0, 2 * ROWS - rest.shape[0]), (0, 0)))
        terms = shape_blocks(shape, g_down)
        for n, start in enumerate(END_DOWN if layer == 0 else TOP_DOWN):
            width = D // (2 * N_DOWN)
            source = ("hbm", terms, (ALL, ALL, ALL, ALL, ALL, pl.ds(n * width, width)))
            entries.append((piece(layer, 1, n, (deep, width), source), start, lag))
        starts = END_IN if layer == 0 else TOP_IN
        for n, start in enumerate(starts):
            for m in (2 * (n % 2), 2 * (n % 2) + 1):
                entries.append((piece(layer, 2, n // 2 * 4 + m, (high, GROUP), ("own", 4, (n // 2, m))), start, lag))
        spills = [
            (ATTEND_POINTS * tile + 2, 4, tile, (4,) + shape.grid + (high, GROUP)) for tile in range(len(starts) // 2, N_IN)]
        total = (5, (2 * ROWS, D)) if layer == 0 else None
        transfer = Scattering(shape, ATTEND_TICKS, entries, spills, total, layer == 0)
        grad, sums_a = attention_backward(
            layer, d_mid, db, hidden, a, vec, mixed, rest, q, k, v, w_in, w_out, shape, transfer, number + 1)
        left = [
            piece(layer, 2, tile * 4 + m, (high, GROUP), ("hbm", transfer.spilled[n], m))
            for n, tile in enumerate(range(len(starts) // 2, N_IN)) for m in range(4)]
        pieces = [one for one in pieces if one not in left]
        number += 2
        rest = rest[:ROWS] + sums_a
    totals = transfer.result.reshape(layers, ROWS, D)[:, : BIAS_U + FF // D].reshape(layers, -1)

    def joined(layer, matrix, pick=lambda i: True):
        found = [one.sum for i, one in enumerate(everything[layer][matrix]) if pick(i)]
        return jnp.concatenate([array[i] for array, i in found], axis=1)

    def joined_in(layer):
        return jnp.concatenate([joined(layer, 2, lambda i, m=m: i % 4 == m) for m in range(3)], axis=1)

    stacked = [
        jnp.stack([joined_in(layer) for layer in range(layers)]),
        jnp.stack([joined(layer, 2, lambda i: i % 4 == 3) for layer in range(layers)]),
        jnp.stack([joined(layer, 0) for layer in range(layers)]),
        jnp.stack([joined(layer, 1) for layer in range(layers)]),
        lax.dynamic_slice_in_dim(totals, mine, vectors.shape[1], axis=1),
    ]
    firsts = (first_attn_in, first_attn_out, first_mlp_in, first_mlp_out, first_vectors)
    seconds = (second_attn_in, second_attn_out, second_mlp_in, second_mlp_out, second_vectors)
    settings = (
        (D ** (-0.5), 0.05),
        ((D // 8) ** (-0.5), 0.05),
        (D ** (-0.5), 0.05),
        (FF ** (-0.5), 0.05),
        (0.3, 0.0),
    )
    updated = [
        adamw(
            shards[member],
            stacked[member],
            firsts[member],
            seconds[member],
            settings[member][0],
            settings[member][1],
        )
        for member in range(5)
    ]
    d_tokens = grad.reshape(images, SPAN, D)[:, :SEQ]
    return (
        output,
        d_tokens,
        updated[0][0],
        updated[1][0],
        updated[2][0],
        updated[3][0],
        updated[4][0],
        updated[0][1],
        updated[1][1],
        updated[2][1],
        updated[3][1],
        updated[4][1],
        updated[0][2],
        updated[1][2],
        updated[2][2],
        updated[3][2],
        updated[4][2],
    )


def solution(mesh):
    in_specs = (
        P(("node", "chip"), None, None),
        P(("node", "chip"), None, None),
        P(None, ("node", "chip"), None),
        P(None, ("node", "chip"), None),
        P(None, ("node", "chip"), None),
        P(None, ("node", "chip"), None),
        P(None, ("node", "chip")),
        P(None, ("node", "chip"), None),
        P(None, ("node", "chip"), None),
        P(None, ("node", "chip"), None),
        P(None, ("node", "chip"), None),
        P(None, ("node", "chip")),
        P(None, ("node", "chip"), None),
        P(None, ("node", "chip"), None),
        P(None, ("node", "chip"), None),
        P(None, ("node", "chip"), None),
        P(None, ("node", "chip")),
    )
    out_specs = (
        P(("node", "chip"), None, None),
        P(("node", "chip"), None, None),
        P(None, ("node", "chip"), None),
        P(None, ("node", "chip"), None),
        P(None, ("node", "chip"), None),
        P(None, ("node", "chip"), None),
        P(None, ("node", "chip")),
        P(None, ("node", "chip"), None),
        P(None, ("node", "chip"), None),
        P(None, ("node", "chip"), None),
        P(None, ("node", "chip"), None),
        P(None, ("node", "chip")),
        P(None, ("node", "chip"), None),
        P(None, ("node", "chip"), None),
        P(None, ("node", "chip"), None),
        P(None, ("node", "chip"), None),
        P(None, ("node", "chip")),
    )
    return jax.shard_map(
        functools.partial(on_device, Shape(mesh)), mesh=mesh, in_specs=in_specs, out_specs=out_specs, check_vma=False
    )
```

```python
import functools
import math

import jax
import jax.numpy as jnp
from jax import lax
from jax.experimental import pallas as pl
from jax.experimental.pallas import tpu as pltpu
from jax.sharding import PartitionSpec as P

STEP = 10
beta_first = 0.9
beta_second = 0.999
adam_eps = 1e-08
MESH = pl.DeviceIdType.MESH
ALL = slice(None)
D = 1024
HEADS = 16
HEAD_DIM = 64
FF = 4096
SEQ = 145
SPAN = 160
GROUP = 256
FF_TILE = 512
ROWS = 16
norm_eps = 1e-06
LOW = jnp.bfloat16
FULL = jnp.float32
GAIN_A, SHIFT_A, BIAS_Q, BIAS_V, BIAS_O, SCALE_A, GAIN_M, SHIFT_M, BIAS_D, SCALE_M, BIAS_U = range(11)


class Shape:
    def __init__(self, mesh):
        chips = mesh.shape["chip"]
        self.X = mesh.shape["node"] // 2
        self.Q = 2 ** ((chips.bit_length() - 1) // 2)
        self.P = chips // self.Q
        self.devices = mesh.shape["node"] * chips
        self.grid = (self.X, 2, self.P, self.Q)
        self.sizes = {"x": self.X, "c": 2, "p": self.P, "q": self.Q}


class Place:
    def __init__(self, shape):
        self.sizes = shape.sizes
        node, chip = lax.axis_index("node"), lax.axis_index("chip")
        self.at = {"x": node // 2, "c": lax.rem(node, 2), "p": chip // shape.Q, "q": lax.rem(chip, shape.Q)}
        self.offs, self.devices = {}, {}
        for axis, n in shape.sizes.items():
            for k in range(1, n):
                off = lax.rem(self.at[axis] + k, n)
                to = dict(self.at, **{axis: off})
                self.offs[axis, k] = off
                self.devices[axis, k] = (to["x"] * 2 + to["c"], to["p"] * shape.Q + to["q"])

    def off(self, axis, k):
        return self.offs[axis, k % self.sizes[axis]]

    def greet(self):
        barrier = pltpu.get_barrier_semaphore()
        for device in self.devices.values():
            pl.semaphore_signal(barrier, inc=1, device_id=device, device_id_type=MESH)
        pl.semaphore_wait(barrier, len(self.devices))


class Move:
    def __init__(self, src, dst, came, sems, device):
        if device is None:
            copy = functools.partial(pltpu.make_async_copy, src, dst, sems[0])
            self.start, self.arrived, self.sent = lambda: copy().start(), lambda: copy().wait(), None
        else:
            copy = functools.partial(
                pltpu.make_async_remote_copy,
                send_sem=sems[0], recv_sem=sems[1], device_id=device, device_id_type=MESH)
            self.start = lambda: copy(src, dst).start()
            self.sent = lambda: copy(src, dst).wait_send()
            self.arrived = lambda: copy(came, came).wait_recv()


class Task:
    def __init__(self, place, sems):
        self.place, self.sems, self.used = place, sems, 0
        self.phases = [([], [], []) for _ in range(5)]

    def move(self, begin, end, src, dst, came=None, axis=None, k=None):
        slot, self.used = self.used, self.used + 1
        sems = (self.sems[0].at[slot], self.sems[1].at[slot])
        move = Move(src, dst, dst if came is None else came, sems, None if axis is None else self.place.devices[axis, k])
        self.phases[begin][2].append(move)
        self.phases[end][0].append(move)


def plan(events):
    todo, flying = {}, []
    for time, task, phase in sorted(events, key=lambda e: (e[0], -e[2])):
        waits, work, starts = task.phases[phase]
        acts = todo.setdefault(time, [])
        acts += [move.arrived for move in waits] + work + [move.start for move in starts]
        acts += [move.sent for move in waits if move.sent is not None]
        flying = [move for move in flying if move not in waits] + starts
    return todo, [move.arrived for move in flying] + [move.sent for move in flying if move.sent is not None]


class Gather(Task):
    def __init__(self, place, src, dst, cols, order, sems):
        super().__init__(place, sems)
        at, sizes = place.at, place.sizes
        one, two, three = order

        def region(**fix):
            pick = dict(at, **fix)
            return dst.at[pick["x"], pick["c"], pick["p"], pick["q"], :, cols]

        def push(begin, end, axis, k, own=None, **held):
            came = region(**dict(held, **{axis: place.off(axis, -k)}))
            self.move(begin, end, region(**held) if own is None else own, region(**held), came, axis, k)

        own = src.at[:, cols]
        self.move(0, 1, own, region())
        for k in range(1, sizes[one]):
            push(0, 1, one, k, own)
        for k in range(1, sizes[two]):
            push(1, 2, two, k, **{one: ALL})
        push(1, 4, "c", 1, **{one: ALL})
        for k in range(1, sizes[three]):
            push(2, 3, three, k, **{one: ALL, two: ALL})
        for k in range(1, sizes[two]):
            push(2, 4, "c", 1, **{one: ALL, two: place.off(two, k)})
        for k in range(1, sizes[three]):
            push(3, 4, "c", 1, **{one: ALL, two: ALL, three: place.off(three, k)})


class Scatter(Task):
    def __init__(self, place, src, acc, out, order, bufs, sems, start, stop):
        super().__init__(place, sems)
        at, sizes = place.at, place.sizes
        self.start, self.stop = start, stop
        left = [a for a in "xpq" if a not in order[: max(start - 1, 0)]]

        def held(**fix):
            x, p, q = [fix.get(a, ALL) for a in "xpq"]
            return src.at[x, at["c"], p, q] if acc is None else acc.at[tuple(fix.get(a, ALL) for a in left)]

        def add(view, terms):
            if len(terms) == 1:
                view[...] = view[...] + terms[0][...]
            else:
                view[...] = sum([term[...].astype(FULL) for term in terms], view[...].astype(FULL)).astype(LOW)

        def finish():
            last = order[2]
            total = held(**at)[...].astype(FULL)
            for k in range(1, sizes[last]):
                total = total + bufs[3][k - 1].astype(FULL)
            out[...] = total

        if start > 0:
            self.move(start - 1, start, src, acc)
        else:
            if acc is not None:
                self.move(0, 1, src.at[:, at["c"]], acc)
            self.move(0, 1, src.at[:, place.off("c", 1)], bufs[0], None, "c", 1)
            for i in range(sizes["x"]):
                self.phases[1][1].append(functools.partial(add, held(x=i), [bufs[0].at[i]]))
        known = {}
        for phase, axis in enumerate(order, 1):
            if phase >= start:
                for k in range(1, sizes[axis]):
                    away = held(**dict(known, **{axis: place.off(axis, k)}))
                    if phase < stop:
                        self.move(phase, phase + 1, away, bufs[phase].at[k - 1], None, axis, k)
            known[axis] = at[axis]
            if start <= phase < min(3, stop):
                terms = [bufs[phase].at[k - 1] for k in range(1, sizes[axis])]
                self.phases[phase + 1][1].append(functools.partial(add, held(**known), terms))
        if stop > 4:
            self.phases[4][1].append(finish)
        self.left_over = held(**{a: at[a] for a in order[: max(stop - 1, 0)]})


class Spill(Task):
    def __init__(self, place, src, dst, sems):
        super().__init__(place, sems)
        self.move(0, 1, src, dst)


class Total(Task):
    def __init__(self, place, src, out, bufs, sems):
        super().__init__(place, sems)
        stages = [src] + list(bufs[4:]) + [out]

        def add(i):
            total = stages[i][...]
            for k in range(1, place.sizes["cxqp"[i]]):
                total = total + bufs[i][k - 1]
            stages[i + 1][...] = total

        for i, axis in enumerate("cxqp"):
            for k in range(1, place.sizes[axis]):
                self.move(i, i + 1, stages[i], bufs[i].at[k - 1], None, axis, k)
            self.phases[i + 1][1].append(functools.partial(add, i))


ANYWHERE = pl.BlockSpec(memory_space=pl.ANY)


ORDERS = (("x", "q", "p"), ("q", "x", "p"))


class Piece:
    def __init__(self, block, source, order):
        self.block, self.source, self.order, self.done, self.sum = block, source, ORDERS[order % len(ORDERS)], 0, None


class Scattering:
    def __init__(self, shape, ticks, entries, spills=(), total=None, last=False):
        self.shape, self.ticks, self.spills, self.total = shape, ticks, spills, total
        self.aliases, self.scratch, self.inputs, self.made = {}, [], [], []
        self.out_shape, self.out_specs = [], []
        sizes = shape.sizes
        blocks = {}
        for piece, tick, lag in entries:
            first = piece.done
            times = {f: tick + lag * f for f in range(5)} if first == 0 else {
                f: tick if f < first else tick + 1 + lag * (f - first) for f in range(first - 1, 5)}
            stop = 5 if last else min([f for f, time in times.items() if time >= ticks] + [5])
            stop = 5 if stop == 4 else stop
            buffers, index = {}, {}
            if piece.source[0] != "own":
                axes = [sizes[a] for a in "xpq" if a not in piece.order[: max(first - 1, 0)]]
                buffers["acc"] = tuple(axes) + piece.block
            if first == 0:
                buffers[0] = tuple(sizes[a] for a in "xpq") + piece.block
            for f, axis in enumerate(piece.order, 1):
                if first <= f < stop:
                    rest = [sizes[a] for a in "xpq" if a not in piece.order[:f]]
                    buffers[f] = (sizes[axis] - 1, *rest) + piece.block
            for key, buffer in buffers.items():
                index[key] = len(self.scratch)
                self.scratch.append(pltpu.VMEM(buffer, LOW))
            if piece.source[0] != "own" and not any(piece.source[1] is a for a in self.inputs):
                self.inputs.append(piece.source[1])
            if stop == 5:
                blocks.setdefault(piece.block, []).append(piece)
            self.made.append([piece, times, stop, index])
        for block, pieces in blocks.items():
            for i, piece in enumerate(pieces):
                piece.target = (len(self.out_shape), i)
            self.out_shape.append(jax.ShapeDtypeStruct((len(pieces),) + block, FULL))
            self.out_specs.append(whole(self.out_shape[-1].shape))
        for piece, _, stop, _ in self.made:
            if stop < 5:
                piece.target = (len(self.out_shape), None)
                axes = [sizes[a] for a in "xpq" if a not in piece.order[: stop - 1]]
                self.out_shape.append(jax.ShapeDtypeStruct(tuple(axes) + piece.block, LOW))
                self.out_specs.append(ANYWHERE)
        self.first_spill = len(self.out_shape)
        for _, _, _, block in spills:
            self.out_shape.append(jax.ShapeDtypeStruct(block, LOW))
            self.out_specs.append(ANYWHERE)
        if total is not None:
            self.first_total = len(self.scratch)
            self.scratch += [pltpu.VMEM((sizes[a] - 1,) + total[1], FULL) for a in "cxqp"]
            self.scratch += [pltpu.VMEM(total[1], FULL)] * 3
            self.out_shape.append(jax.ShapeDtypeStruct(total[1], FULL))
            self.out_specs.append(whole(total[1]))
        self.in_specs = [ANYWHERE] * len(self.inputs)
        copies = max(3 + sum(sizes[a] - 1 for a in "xpq"), sum(n - 1 for n in sizes.values()))
        self.scratch += [pltpu.SemaphoreType.DMA((len(self.made) + len(spills) + 1, copies))] * 2

    def build(self, ins, outs, scratch, own):
        place = Place(self.shape)
        send, recv = scratch[-2:]
        events, halted, slot = [], [], 0
        for piece, times, stop, index in self.made:
            kind, base, lead = piece.source
            if kind == "own":
                src = own[base].at[lead]
            else:
                src = ins[[a is base for a in self.inputs].index(True)]
                src = src if lead is None else src.at[lead]
            bufs = {key: scratch[i] for key, i in index.items()}
            o, i = piece.target
            out = outs[o].at[i] if stop == 5 else outs[o]
            task = Scatter(
                place, src, bufs.get("acc"), out, piece.order, bufs, (send.at[slot], recv.at[slot]), piece.done, stop)
            slot += 1
            events += [(time, task, f) for f, time in times.items() if f < stop]
            if stop < 5:
                halted.append((task, out))
        for n, (tick, base, lead, _) in enumerate(self.spills):
            task = Spill(place, own[base].at[lead], outs[self.first_spill + n], (send.at[slot], recv.at[slot]))
            slot += 1
            events.append((tick, task, 0))
        if self.total is not None:
            task = Total(
                place, own[self.total[0]], outs[-1], scratch[self.first_total : -2], (send.at[slot], recv.at[slot]))
            events += [(self.ticks + 2 * f, task, f) for f in range(5)]
        todo, rest = plan(events)
        moves = []
        for task, out in halted:
            rest += task.phases[task.stop][1]
            move = Move(task.left_over, out, None, (task.sems[0].at[task.used],), None)
            rest.append(move.start)
            moves.append(move.arrived)
        return place, todo, rest + moves

    def take(self, outs):
        for piece, _, stop, _ in self.made:
            o, i = piece.target
            if stop == 5:
                piece.sum = (outs[o], i)
            else:
                piece.source, piece.done = ("part", outs[o], None), stop
        self.spilled = outs[self.first_spill : self.first_spill + len(self.spills)]
        self.result = outs[-1]


def beside(kernel, points, transfer, number, grid, inputs, in_specs, out_specs, out_shape, scratch, name, limit=62):
    total = grid * points
    counts = [len(inputs), len(transfer.inputs) if transfer else 0, len(out_shape), len(transfer.out_shape) if transfer else 0, len(scratch)]

    def body(*refs):
        groups, i = [], 0
        for n in counts:
            groups.append(refs[i : i + n])
            i += n
        groups.append(refs[i:])
        step = pl.program_id(0)
        if transfer is None:
            kernel(lambda point: None, *groups[0], *groups[2], *groups[4])
            return
        place, todo, rest = transfer.build(groups[1], groups[3], groups[5], groups[4])

        def tick(point):
            if point == 0:
                pl.when(step == 0)(place.greet)
            for time in sorted(todo):
                if time < total and time % points == point:
                    @pl.when(step == time // points)
                    def _():
                        for act in todo[time]:
                            act()

        kernel(tick, *groups[0], *groups[2], *groups[4])

        @pl.when(step == grid - 1)
        def _():
            for act in [act for time in sorted(todo) if time >= total for act in todo[time]] + rest:
                act()

    extra = {}
    if transfer is not None:
        extra["input_output_aliases"] = {counts[0] + i: counts[2] + o for i, o in transfer.aliases.items()}
        inputs, in_specs = list(inputs) + transfer.inputs, list(in_specs) + transfer.in_specs
        out_specs, out_shape = list(out_specs) + transfer.out_specs, list(out_shape) + transfer.out_shape
        scratch = list(scratch) + transfer.scratch
    outs = pl.pallas_call(
        body,
        grid=(grid,),
        in_specs=in_specs,
        out_specs=out_specs,
        out_shape=out_shape,
        scratch_shapes=scratch,
        name=name,
        compiler_params=pltpu.CompilerParams(
            dimension_semantics=("arbitrary",),
            vmem_limit_bytes=limit * 2**20,
            collective_id=None if transfer is None else number,
            has_side_effects=transfer is not None,
        ),
        **extra,
    )(*inputs)
    if transfer is not None:
        transfer.take(outs[counts[2] :])
    return outs[: counts[2]]


def mul(a, b):
    return jnp.dot(a, b, preferred_element_type=FULL)


def mul_nt(a, b):
    return lax.dot_general(a, b, (((1,), (1,)), ((), ())), preferred_element_type=FULL)


def mul_tn(a, b):
    return lax.dot_general(a, b, (((0,), (0,)), ((), ())), preferred_element_type=FULL)


def normalise(values):
    centred = values - jnp.mean(values, axis=-1, keepdims=True)
    inverse = lax.rsqrt(jnp.mean(centred * centred, axis=-1, keepdims=True) + norm_eps)
    return centred * inverse, inverse


def tiles(rows, step=160):
    return [slice(i, i + step) for i in range(0, rows, step)]


def fill_rows(rows, tokens):
    rows[...] = jnp.zeros_like(rows)
    for i in range(tokens.shape[0]):
        rows[i * SPAN : i * SPAN + SEQ, :] = tokens[i].astype(FULL)


def row(vec, index):
    return vec[index : index + 1, :]


def softmax_of(q, k, lanes, width):
    scores = mul_nt(jnp.where(lanes, q, jnp.zeros_like(q)), k) * HEAD_DIM ** (-0.5)
    scores = jnp.where(width, scores, -1e30)
    expo = jnp.exp(scores - jnp.max(scores, axis=-1, keepdims=True))
    return expo * (1.0 / jnp.sum(expo, axis=-1, keepdims=True))


def lane_sets():
    lane = lax.broadcasted_iota(jnp.int32, (SPAN, 128), 1)
    return [lane < HEAD_DIM, lane >= HEAD_DIM]


def key_set():
    return lax.broadcasted_iota(jnp.int32, (SPAN, SPAN), 1) < SEQ


def whole(shape):
    return pl.BlockSpec(shape, lambda j: (0,) * len(shape), pipeline_mode=pl.Buffered(1))


def whole_of(layer, rows):
    return pl.BlockSpec((None, rows, D), lambda j: (layer, 0, 0), pipeline_mode=pl.Buffered(1))


def columns_of(layer, rows, width):
    return pl.BlockSpec((None, rows, width), lambda j: (layer, 0, j))


def columns(rows, width, at=0):
    return pl.BlockSpec((rows, width), lambda j: (0, j + at))


def lines(height, cols):
    return pl.BlockSpec((height, cols), lambda j: (j, 0))


def phi_of(u):
    return 0.5 * (1.0 + lax.erf(u * 0.5**0.5))


N_IN, N_UP, N_DOWN = D // GROUP, FF // FF_TILE, D // GROUP
ITEMS = N_IN + 1 + N_UP + N_DOWN
GATHER_LAG = 3
AHEAD = 4 * GATHER_LAG + 1
GATHER_ORDERS = (("p", "q", "x"), ("p", "x", "q")) * 2 + (("q", "p", "x"), ("x", "p", "q"))


def item_of(number):
    if number < N_IN:
        return 0, number, pl.ds(number * 3 * GROUP, 3 * GROUP)
    number -= N_IN
    if number == 0:
        return 1, 0, pl.ds(0, D)
    number -= 1
    if number < N_UP:
        return 2, number, pl.ds(number * FF_TILE, FF_TILE)
    return 3, number - N_UP, pl.ds((number - N_UP) * GROUP, GROUP)


def matrix_of(ref):
    value = ref[...]
    flat = (-1, value.shape[-1])
    return value.reshape(flat) if value.shape[-2] % 16 == 0 else value.astype(FULL).reshape(flat).astype(LOW)


def forward_kernel(shape, layers, *refs):
    count = 4 * layers
    tokens, packed, *sources = refs[: 2 + count]
    refs = refs[2 + count :]
    a_out, q_out, k_out, v_out, mixed_out, branch_out, mid_out, c_out, u_out, act_out, down_out, hidden_out, vec_out, low_out = refs[:14]
    gathered, refs = refs[14 : 14 + count], refs[14 + count :]
    h, act, vec = refs[:3]
    slots, sums, (send, recv, loaded) = refs[3:7], refs[7:14], refs[14:]
    step = pl.program_id(0)
    rows = h.shape[0]
    place = Place(shape)
    total = layers * ITEMS
    jobs, loads, n = [], [], 1
    for layer in range(layers):
        for number in range(ITEMS):
            weight, index, cols = item_of(number)
            src, dst = sources[4 * layer + weight], gathered[4 * layer + weight]
            half, job = cols.size // 2, []
            for i in range(2):
                part = pl.ds(cols.start + i * half, half)
                order = GATHER_ORDERS[(n - 1) % len(GATHER_ORDERS)]
                job.append(Gather(place, src, dst, part, order, (send.at[n], recv.at[n])))
                n += 1
            jobs.append(job)
            slot = index % slots[weight].shape[0]
            loads.append(
                functools.partial(
                    pltpu.make_async_copy, dst.at[:, :, :, :, :, cols], slots[weight].at[slot], loaded.at[weight, slot]))
    jobs[0].append(Total(place, packed, vec_out, sums, (send.at[0], recv.at[0])))
    todo, _ = plan([
        (i + GATHER_LAG * phase, task, phase) for i, job in enumerate(jobs) for task in job for phase in range(5)])

    pl.when(step == 0)(place.greet)
    for s in range(total + AHEAD):
        @pl.when(step == s)
        def _():
            if 0 <= s - AHEAD < total:
                loads[s - AHEAD]().wait()
            for act in todo.get(s, []):
                act()
            if 0 <= s - AHEAD + 1 < total:
                loads[s - AHEAD + 1]().start()

    at = step - AHEAD
    item = jnp.maximum(lax.rem(jnp.maximum(at, 0), ITEMS), 0)
    layer = jnp.maximum(at, 0) // ITEMS
    live = at >= 0
    base = pl.multiple_of(layer * ROWS, ROWS)

    def line(index):
        return vec[pl.ds(index, 1), :]

    @pl.when(at == 0)
    def _():
        fill_rows(h, tokens)

    @pl.when(live & (item == 0))
    def _():
        vec[...] = vec_out[pl.ds(base, ROWS), :]
        hidden_out[0] = h[...]
        for t in tiles(rows):
            normal, _ = normalise(h[t, :])
            a_out[0, t, :] = (normal * line(GAIN_A) + line(SHIFT_A)).astype(LOW)

    @pl.when(live & (item < N_IN))
    def _():
        group = pl.ds(pl.multiple_of(item * GROUP, GROUP), GROUP)
        proj = mul(a_out[0], matrix_of(slots[0].at[lax.rem(item, 2)]))
        q_out[0] = (proj[:, :GROUP] + vec[BIAS_Q : BIAS_Q + 1, group]).astype(LOW)
        k_out[0] = proj[:, GROUP : 2 * GROUP].astype(LOW)
        v_out[0] = (proj[:, 2 * GROUP :] + vec[BIAS_V : BIAS_V + 1, group]).astype(LOW)
        lanes, width = lane_sets(), key_set()

        def image(i, carry):
            t = pl.ds(pl.multiple_of(i * SPAN, SPAN), SPAN)
            done = []
            for pair in range(GROUP // 128):
                cols = slice(pair * 128, pair * 128 + 128)
                q, k, v = q_out[0, t, cols], k_out[0, t, cols], v_out[0, t, cols]
                both = [mul(softmax_of(q, k, lanes[s], width).astype(LOW), v) for s in range(2)]
                done.append(jnp.where(lanes[0], both[0], both[1]).astype(LOW))
            mixed_out[0, t, group] = jnp.concatenate(done, axis=1)
            return carry

        lax.fori_loop(0, rows // SPAN, image, 0)

    @pl.when(live & (item == N_IN))
    def _():
        weight = matrix_of(slots[1].at[0])
        for t in tiles(rows):
            branch = mul(mixed_out[0, t, :], weight) + line(BIAS_O)
            branch_out[0, t, :] = branch
            middle = h[t, :] + line(SCALE_A) * branch
            mid_out[0, t, :] = middle
            normal, _ = normalise(middle)
            c_out[0, t, :] = (normal * line(GAIN_M) + line(SHIFT_M)).astype(LOW)

    @pl.when(live & (item > N_IN) & (item <= N_IN + N_UP))
    def _():
        tile = item - N_IN - 1
        per = D // FF_TILE
        bias = vec[pl.ds(BIAS_U + tile // per, 1), pl.ds(pl.multiple_of(lax.rem(tile, per) * FF_TILE, FF_TILE), FF_TILE)]
        u = mul(c_out[0], matrix_of(slots[2].at[lax.rem(tile, 2)])) + bias
        u_out[0] = u
        active = (u * phi_of(u)).astype(LOW)
        act_out[0] = active
        act[:, pl.ds(pl.multiple_of(tile * FF_TILE, FF_TILE), FF_TILE)] = active

    @pl.when(live & (item > N_IN + N_UP))
    def _():
        tile = item - N_IN - 1 - N_UP
        group = pl.ds(pl.multiple_of(tile * GROUP, GROUP), GROUP)
        down = mul(act[...], matrix_of(slots[3].at[lax.rem(tile, 2)])) + vec[BIAS_D : BIAS_D + 1, group]
        down_out[0, :, group] = down
        h[:, group] = mid_out[0, :, group] + vec[SCALE_M : SCALE_M + 1, group] * down

    @pl.when(at == total - 1)
    def _():
        for i in range(low_out.shape[0]):
            low_out[i] = h[i * SPAN : i * SPAN + SEQ, :].astype(LOW)


def forward(shape, layers, tokens, packed, sources, number):
    rows = tokens.shape[0] * SPAN
    total = layers * ITEMS

    def spot(s):
        at = jnp.clip(s - AHEAD, 0, total - 1)
        return at // ITEMS, lax.rem(at, ITEMS)

    def out(width, dtype, pick=None, block=D):
        def index(s):
            layer, item = spot(s)
            return layer, 0, 0 if pick is None else pick(item)

        return jax.ShapeDtypeStruct((layers, rows, width), dtype), pl.BlockSpec((1, rows, block), index)

    def one(spec_shape, dtype):
        return jax.ShapeDtypeStruct(spec_shape, dtype), whole(spec_shape)

    group = lambda item: jnp.minimum(item, N_IN - 1)
    tile = lambda item: jnp.clip(item - N_IN - 1, 0, N_UP - 1)
    qkv = [out(D, LOW, group, GROUP)] * 3
    outs = [out(D, LOW)] + qkv + [out(D, LOW), out(D, FULL), out(D, FULL), out(D, LOW)]
    outs += [out(FF, FULL, tile, FF_TILE), out(FF, LOW, tile, FF_TILE), out(D, FULL), out(D, FULL)]
    outs += [one(packed.shape, FULL), one(tokens.shape, LOW)]
    outs += [(jax.ShapeDtypeStruct(shape.grid + b.shape, LOW), ANYWHERE) for b in sources]
    sizes = shape.sizes
    tasks = 2 * total + 1
    copies = 1 + sum(sizes[a] - 1 for a in "xpq") + 1 + 2 * (max(sizes.values()) - 1)
    deep = [b.shape[0] for b in sources[:4]]
    slots = [
        pltpu.VMEM((count,) + shape.grid + (depth, width), LOW)
        for count, depth, width in zip((2, 1, 2, 2), deep, (3 * GROUP, D, FF_TILE, GROUP))
    ]
    return pl.pallas_call(
        functools.partial(forward_kernel, shape, layers),
        grid=(total + AHEAD,),
        in_specs=[whole(tokens.shape), whole(packed.shape)] + [ANYWHERE] * len(sources),
        out_specs=[o[1] for o in outs],
        out_shape=[o[0] for o in outs],
        scratch_shapes=[pltpu.VMEM((rows, D), FULL), pltpu.VMEM((rows, FF), LOW), pltpu.VMEM((ROWS, D), FULL)]
        + slots
        + [pltpu.VMEM((sizes[a] - 1,) + packed.shape, FULL) for a in "cxqp"]
        + [pltpu.VMEM(packed.shape, FULL)] * 3
        + [pltpu.SemaphoreType.DMA((tasks, copies))] * 2
        + [pltpu.SemaphoreType.DMA((4, 2))],
        name="forward",
        compiler_params=pltpu.CompilerParams(
            dimension_semantics=("arbitrary",), vmem_limit_bytes=60 * 2**20, collective_id=number, has_side_effects=True),
    )(tokens, packed, *sources)


def norm_back(values, upstream, gain):
    normal, inverse = normalise(values)
    scaled = upstream * gain
    inner = (
        scaled
        - jnp.mean(scaled, axis=-1, keepdims=True)
        - normal * jnp.mean(scaled * normal, axis=-1, keepdims=True)
    )
    return inverse * inner, upstream * normal


def summed(values):
    return jnp.sum(values, axis=0, keepdims=True)


def mlp_bwd(tick, given, down, mid, branch, c, vec, u, act, wu, wd, g_down, d_mid, db_out, sums, d_bias_u, dd, stage, *own):
    step, last = pl.program_id(0), pl.num_programs(0) - 1
    rows = mid.shape[0]
    g = own[0] if own else given
    tick(0)

    @pl.when(step == 0)
    def _():
        sums[...] = jnp.zeros_like(sums)
        if own:
            fill_rows(g, given)
        for t in tiles(rows):
            grad = g[t, :]
            scaled = grad * row(vec, SCALE_M)
            sums[SCALE_M : SCALE_M + 1, :] += summed(grad * down[t, :])
            sums[BIAS_D : BIAS_D + 1, :] += summed(scaled)
            dd[t, :] = scaled.astype(LOW)
        d_mid[...] = jnp.zeros_like(d_mid)

    d_act = mul_nt(dd[...], wd[...])
    upper = u[...]
    density = jnp.exp(-0.5 * upper * upper) * (2.0 * math.pi) ** (-0.5)
    du = d_act * (phi_of(upper) + upper * density)
    d_bias_u[...] = summed(du)
    du_b = du.astype(LOW)
    stage[step] = mul_tn(c[...], du_b).reshape(stage.shape[1:]).astype(LOW)
    tick(1)
    g_down[...] = mul_tn(act[...], dd[...]).astype(LOW)
    d_mid[...] += mul_nt(du_b, wu[...])

    @pl.when(step == last)
    def _():
        for t in tiles(rows):
            upstream = d_mid[t, :]
            through, gain_terms = norm_back(mid[t, :], upstream, row(vec, GAIN_M))
            sums[GAIN_M : GAIN_M + 1, :] += summed(gain_terms)
            sums[SHIFT_M : SHIFT_M + 1, :] += summed(upstream)
            middle = g[t, :] + through
            d_mid[t, :] = middle
            sums[SCALE_A : SCALE_A + 1, :] += summed(middle * branch[t, :])
            db = middle * row(vec, SCALE_A)
            sums[BIAS_O : BIAS_O + 1, :] += summed(db)
            db_out[t, :] = db.astype(LOW)


def mlp_backward(layer, g, down, mid, branch, c, vec, u, act, w_up, w_down, shape, transfer, number):
    rows = mid.shape[1]
    f32, low = lambda s: jax.ShapeDtypeStruct(s, FULL), lambda s: jax.ShapeDtypeStruct(s, LOW)
    full = whole((rows, D))
    tile = columns_of(layer, rows, FF_TILE)
    steps = FF // FF_TILE
    return beside(
        mlp_bwd,
        points=MLP_POINTS,
        transfer=transfer,
        number=number,
        grid=steps,
        inputs=[g, down, mid, branch, c, vec, u, act, w_up, w_down],
        in_specs=[whole(g.shape)] + [whole_of(layer, rows)] * 4
        + [whole(vec.shape), tile, tile, columns(D, FF_TILE), lines(FF_TILE, D)],
        out_specs=[lines(FF_TILE, D), full, full, whole((ROWS, D)), columns(1, FF_TILE)],
        out_shape=[low((FF, D)), f32((rows, D)), low((rows, D)), f32((ROWS, D)), f32((1, FF))],
        scratch=[
            pltpu.VMEM((rows, D), LOW),
            pltpu.VMEM((steps,) + shape.grid + (D // shape.devices, FF_TILE), LOW),
        ]
        + [pltpu.VMEM((rows, D), FULL)] * (g.ndim == 3),
        name="mlp_backward",
    )


def attend_bwd(tick, d_mid, db, h, a, vec, mixed, rest, q, k, v, wq, wk, wv, wo, g_out, sums, dq, dk, dv, dm, stage, values):
    step, last = pl.program_id(0), pl.num_programs(0) - 1
    rows = h.shape[0]
    tick(0)

    @pl.when(step == 0)
    def _():
        sums[...] = jnp.zeros_like(sums)
        g_out[...] = jnp.zeros_like(g_out)

    def store(kind, term):
        stage[step, kind] = term.reshape(stage.shape[2:]).astype(LOW)

    group = pl.ds(pl.multiple_of(step * GROUP, GROUP), GROUP)
    dm[...] = mul_nt(db[...], wo[...]).astype(LOW)
    store(3, mul_tn(mixed[...], db[:, group]))
    lanes, width = lane_sets(), key_set()

    def image(i, carry):
        at = pl.ds(pl.multiple_of(i * SPAN, SPAN), SPAN)
        bias = []
        for pair in range(GROUP // 128):
            cols = slice(pair * 128, pair * 128 + 128)
            qp, kp, vp, dmp = q[at, cols], k[at, cols], v[at, cols], dm[at, cols]
            grads = []
            for s in range(2):
                prob = softmax_of(qp, kp, lanes[s], width)
                d_prob = mul_nt(jnp.where(lanes[s], dmp, jnp.zeros_like(dmp)), vp)
                ds = (prob * (d_prob - jnp.sum(prob * d_prob, axis=-1, keepdims=True))).astype(LOW)
                grads.append((mul(ds, kp), mul_tn(ds, qp), mul_tn(prob.astype(LOW), dmp)))
            d_q, d_k, d_v = [jnp.where(lanes[0], one, two) for one, two in zip(*grads)]
            d_q, d_k = d_q * HEAD_DIM ** (-0.5), d_k * HEAD_DIM ** (-0.5)
            dq[at, cols], dk[at, cols], dv[at, cols] = d_q.astype(LOW), d_k.astype(LOW), d_v.astype(LOW)
            bias.append((summed(d_q), summed(d_v)))
        sums[BIAS_Q : BIAS_Q + 1, group] += jnp.concatenate([b[0] for b in bias], axis=1)
        sums[BIAS_V : BIAS_V + 1, group] += jnp.concatenate([b[1] for b in bias], axis=1)
        return carry

    images = rows // SPAN
    lax.fori_loop(0, images // 2, image, 0)
    tick(1)
    lax.fori_loop(images // 2, images, image, 0)
    for kind, term in enumerate((dq, dk, dv)):
        store(kind, mul_tn(a[...], term[...]))
    tick(2)
    g_out[...] += mul_nt(dq[...], wq[...]) + mul_nt(dk[...], wk[...]) + mul_nt(dv[...], wv[...])

    @pl.when(step == last)
    def _():
        for t in tiles(rows):
            upstream = g_out[t, :]
            through, gain_terms = norm_back(h[t, :], upstream, row(vec, GAIN_A))
            sums[GAIN_A : GAIN_A + 1, :] += summed(gain_terms)
            sums[SHIFT_A : SHIFT_A + 1, :] += summed(upstream)
            g_out[t, :] = d_mid[t, :] + through
        values[...] = rest[...]
        values[:ROWS, :] += sums[...]


def attention_backward(layer, d_mid, db, h, a, vec, mixed, rest, q, k, v, w_in, w_out, shape, transfer, number):
    rows = d_mid.shape[0]
    n = D // GROUP
    f32 = lambda s: jax.ShapeDtypeStruct(s, FULL)
    full = whole((rows, D))
    cols = columns_of(layer, rows, GROUP)
    return beside(
        attend_bwd,
        points=ATTEND_POINTS,
        transfer=transfer,
        number=number,
        grid=n,
        inputs=[d_mid, db, h, a, vec, mixed, rest, q, k, v, w_in, w_in, w_in, w_out],
        in_specs=[full] * 2
        + [whole_of(layer, rows)] * 2
        + [whole(vec.shape), whole_of(layer, rows), whole(rest.shape)]
        + [cols] * 3
        + [pl.BlockSpec((D, GROUP), lambda j, m=m: (0, 3 * j + m)) for m in range(3)]
        + [lines(GROUP, D)],
        out_specs=[full, whole((ROWS, D))],
        out_shape=[f32((rows, D)), f32((ROWS, D))],
        scratch=[pltpu.VMEM((rows, GROUP), LOW)] * 4
        + [
            pltpu.VMEM((n, 4) + shape.grid + (D // shape.devices, GROUP), LOW),
            pltpu.VMEM(rest.shape, FULL),
        ],
        name="attention_backward",
    )


MLP_POINTS, MLP_LAG = 2, 3
ATTEND_POINTS = 3
TOP_LAG = 2
END_LAG = 2
MLP_TICKS, ATTEND_TICKS = MLP_POINTS * N_UP, ATTEND_POINTS * N_IN
TOP_UP = (1, 3, 5, 7, 9, 11, 13, 15)
TOP_DOWN = (1, 2, 5, 6, 9, 10, 11, 11)
TOP_IN = (3, 4, 7, 8)
LOW_LEFT = (2, 3, 5, 6)
LOW_UP = (7, 9, 11, 13, 14, 15)
END_LEFT = (1, 2)
END_DOWN = (2, 3, 5, 6, 8, 9, 10, 10)
END_IN = (4, 4, 7, 7, 9, 9, 11, 11)


def resumed(pieces, lag):
    under_way = [piece for piece in pieces if piece.sum is None]
    return [(piece, i // 8, lag) for i, piece in enumerate(under_way)]


def shape_blocks(shape, term):
    return term.reshape(shape.grid + (term.shape[0] // shape.devices, term.shape[1]))


def adamw(weight, gradient, first, second, rate, decay):
    first_new = beta_first * first + (1.0 - beta_first) * gradient
    second_new = beta_second * second + (1.0 - beta_second) * gradient * gradient
    fix_first = 1.0 - beta_first**STEP
    fix_second = 1.0 - beta_second**STEP
    stepped = first_new / fix_first / (jnp.sqrt(second_new / fix_second) + adam_eps)
    return (weight - rate * (stepped + decay * weight), first_new, second_new)


def on_device(
    shape,
    tokens,
    cotangent,
    w_attn_in,
    w_attn_out,
    w_mlp_in,
    w_mlp_out,
    vectors,
    first_attn_in,
    first_attn_out,
    first_mlp_in,
    first_mlp_out,
    first_vectors,
    second_attn_in,
    second_attn_out,
    second_mlp_in,
    second_mlp_out,
    second_vectors,
):
    shards = (w_attn_in, w_attn_out, w_mlp_in, w_mlp_out, vectors)
    layers, images = w_attn_in.shape[0], tokens.shape[0]
    mine = lax.axis_index(("node", "chip")) * vectors.shape[1]
    entries = D * (BIAS_U + FF // D)
    packed = lax.dynamic_update_slice_in_dim(
        jnp.zeros((layers, entries), FULL), lax.reduce_precision(vectors, 8, 7), mine, axis=1)
    packed = jnp.pad(packed, ((0, 0), (0, D * ROWS - entries))).reshape(layers * ROWS, D)
    sources = []
    for layer in range(layers):
        by_group = shards[0][layer].reshape(-1, 3, D // GROUP, GROUP).transpose(0, 2, 1, 3).reshape(-1, 3 * D)
        sources += [m.astype(LOW) for m in (by_group, w_attn_out[layer], w_mlp_in[layer], w_mlp_out[layer])]
    outs = forward(shape, layers, tokens, packed, sources, 1)
    hidden, vec_rows, low = outs[11:14]
    weights = [w.reshape(-1, w.shape[-1]) for w in outs[14:]]
    kept = []
    for layer in range(layers):
        a, q, k, v, mixed, branch, mid, c, u, act, down = outs[:11]
        vec = vec_rows[layer * ROWS : layer * ROWS + ROWS]
        kept.append((vec, *weights[4 * layer : 4 * layer + 4], hidden, a, q, k, v, mixed, branch, mid, c, u, act, down))
    grad = cotangent
    high, deep = D // shape.devices, FF // shape.devices
    pieces, rest, left, number, order = [], jnp.zeros((0, D), FULL), [], 10, 0
    everything = [[[None] * (2 * N_UP), [None] * N_DOWN * 2, [None] * 4 * N_IN] for _ in range(layers)]

    def piece(layer, matrix, index, block, source):
        made = everything[layer][matrix][index] = Piece(block, source, index)
        pieces.append(made)
        return made

    for layer in reversed(range(layers)):
        vec, w_in, w_out, w_up, w_down, hidden, a, q, k, v, mixed, branch, mid, c, u, act, down = kept[layer]
        top = layer == layers - 1
        entries = resumed(pieces, MLP_LAG)
        for i, one in enumerate(left):
            entries.append((one, LOW_LEFT[i // 2], MLP_LAG))
        starts = TOP_UP if top else LOW_UP
        half = FF_TILE // 2
        for tile, start in enumerate(starts):
            for i in range(2):
                source = ("own", 1, (tile, ALL, ALL, ALL, ALL, ALL, pl.ds(i * half, half)))
                entries.append((piece(layer, 0, 2 * tile + i, (high, half), source), start, MLP_LAG))
        spills = [
            (MLP_TICKS, 1, tile, shape.grid + (high, FF_TILE)) for tile in range(len(starts), N_UP)]
        transfer = Scattering(shape, MLP_TICKS, entries, spills)
        g_down, d_mid, db, sums_m, d_bias_u = mlp_backward(
            layer, grad, down, mid, branch, c, vec, u, act, w_up, w_down, shape, transfer, number)
        lag = TOP_LAG if layer else END_LAG
        entries = resumed(pieces, lag)
        for n, tile in enumerate(range(len(starts), N_UP)):
            for i in range(2):
                source = ("hbm", transfer.spilled[n], (ALL, ALL, ALL, ALL, ALL, pl.ds(i * half, half)))
                entries.append((piece(layer, 0, 2 * tile + i, (high, half), source), END_LEFT[n], lag))
        spare = jnp.zeros((ROWS - BIAS_U - FF // D, D), FULL)
        rest = jnp.concatenate([sums_m[:BIAS_U], d_bias_u.reshape(-1, D), spare, rest])
        rest = jnp.pad(rest, ((0, 2 * ROWS - rest.shape[0]), (0, 0)))
        terms = shape_blocks(shape, g_down)
        for n, start in enumerate(END_DOWN if layer == 0 else TOP_DOWN):
            width = D // (2 * N_DOWN)
            source = ("hbm", terms, (ALL, ALL, ALL, ALL, ALL, pl.ds(n * width, width)))
            entries.append((piece(layer, 1, n, (deep, width), source), start, lag))
        starts = END_IN if layer == 0 else TOP_IN
        for n, start in enumerate(starts):
            for m in (2 * (n % 2), 2 * (n % 2) + 1):
                entries.append((piece(layer, 2, n // 2 * 4 + m, (high, GROUP), ("own", 4, (n // 2, m))), start, lag))
        spills = [
            (ATTEND_POINTS * tile + 2, 4, tile, (4,) + shape.grid + (high, GROUP)) for tile in range(len(starts) // 2, N_IN)]
        total = (5, (2 * ROWS, D)) if layer == 0 else None
        transfer = Scattering(shape, ATTEND_TICKS, entries, spills, total, layer == 0)
        grad, sums_a = attention_backward(
            layer, d_mid, db, hidden, a, vec, mixed, rest, q, k, v, w_in, w_out, shape, transfer, number + 1)
        left = [
            piece(layer, 2, tile * 4 + m, (high, GROUP), ("hbm", transfer.spilled[n], m))
            for n, tile in enumerate(range(len(starts) // 2, N_IN)) for m in range(4)]
        pieces = [one for one in pieces if one not in left]
        number += 2
        rest = rest[:ROWS] + sums_a
    totals = transfer.result.reshape(layers, ROWS, D)[:, : BIAS_U + FF // D].reshape(layers, -1)

    def joined(layer, matrix, pick=lambda i: True):
        found = [one.sum for i, one in enumerate(everything[layer][matrix]) if pick(i)]
        return jnp.concatenate([array[i] for array, i in found], axis=1)

    def joined_in(layer):
        return jnp.concatenate([joined(layer, 2, lambda i, m=m: i % 4 == m) for m in range(3)], axis=1)

    stacked = [
        jnp.stack([joined_in(layer) for layer in range(layers)]),
        jnp.stack([joined(layer, 2, lambda i: i % 4 == 3) for layer in range(layers)]),
        jnp.stack([joined(layer, 0) for layer in range(layers)]),
        jnp.stack([joined(layer, 1) for layer in range(layers)]),
        lax.dynamic_slice_in_dim(totals, mine, vectors.shape[1], axis=1),
    ]
    firsts = (first_attn_in, first_attn_out, first_mlp_in, first_mlp_out, first_vectors)
    seconds = (second_attn_in, second_attn_out, second_mlp_in, second_mlp_out, second_vectors)
    settings = (
        (D ** (-0.5), 0.05),
        ((D // 8) ** (-0.5), 0.05),
        (D ** (-0.5), 0.05),
        (FF ** (-0.5), 0.05),
        (0.3, 0.0),
    )
    updated = [
        adamw(
            shards[member],
            stacked[member],
            firsts[member],
            seconds[member],
            settings[member][0],
            settings[member][1],
        )
        for member in range(5)
    ]
    d_tokens = grad.reshape(images, SPAN, D)[:, :SEQ]
    return (
        low,
        d_tokens,
        updated[0][0],
        updated[1][0],
        updated[2][0],
        updated[3][0],
        updated[4][0],
        updated[0][1],
        updated[1][1],
        updated[2][1],
        updated[3][1],
        updated[4][1],
        updated[0][2],
        updated[1][2],
        updated[2][2],
        updated[3][2],
        updated[4][2],
    )


def solution(mesh):
    in_specs = (
        P(("node", "chip"), None, None),
        P(("node", "chip"), None, None),
        P(None, ("node", "chip"), None),
        P(None, ("node", "chip"), None),
        P(None, ("node", "chip"), None),
        P(None, ("node", "chip"), None),
        P(None, ("node", "chip")),
        P(None, ("node", "chip"), None),
        P(None, ("node", "chip"), None),
        P(None, ("node", "chip"), None),
        P(None, ("node", "chip"), None),
        P(None, ("node", "chip")),
        P(None, ("node", "chip"), None),
        P(None, ("node", "chip"), None),
        P(None, ("node", "chip"), None),
        P(None, ("node", "chip"), None),
        P(None, ("node", "chip")),
    )
    out_specs = (
        P(("node", "chip"), None, None),
        P(("node", "chip"), None, None),
        P(None, ("node", "chip"), None),
        P(None, ("node", "chip"), None),
        P(None, ("node", "chip"), None),
        P(None, ("node", "chip"), None),
        P(None, ("node", "chip")),
        P(None, ("node", "chip"), None),
        P(None, ("node", "chip"), None),
        P(None, ("node", "chip"), None),
        P(None, ("node", "chip"), None),
        P(None, ("node", "chip")),
        P(None, ("node", "chip"), None),
        P(None, ("node", "chip"), None),
        P(None, ("node", "chip"), None),
        P(None, ("node", "chip"), None),
        P(None, ("node", "chip")),
    )
    return jax.shard_map(
        functools.partial(on_device, Shape(mesh)), mesh=mesh, in_specs=in_specs, out_specs=out_specs, check_vma=False
    )
```
